512 devices in a mesh: ctx: 32 (over y, x), mp: 16 (over z, core).
Axes of the slice: x: 4, y: 8, z: 8, core: 2. Of those that a mesh axis runs over, the one named last changes fastest.
Arguments:
- gate_in: bfloat16 [4096, 8192], P('ctx', 'mp'), may hold values from -6 to 6
- value_in: bfloat16 [4096, 8192], P('ctx', 'mp'), may hold values from -6 to 6
- gate_out: bfloat16 [4096, 8192], P('ctx', 'mp'), may hold values from -7 to 7
- filter_taps: float32 [4096, 8192], P('ctx', 'mp'), may hold values from -1 to 1
- skip_gain: float32 [8192], P('mp'), may hold values from 0.1 to 1.9
- queries: bfloat16 [4096, 8192], P('ctx', 'mp'), may hold values from -8 to 8
- key_rows: bfloat16 [4096, 8192], P('ctx', 'mp'), may hold values from -8 to 8
Outputs:
- mixer_out: bfloat16 [4096, 8192], P('ctx', 'mp')
- attended: bfloat16 [4096, 8192], P('ctx', 'mp')
The draws below stay inside these ranges and needn't reach their ends.
All inputs are finite; a program needn't handle non-finite values.
Results may differ from the reference program's by a relative error of at most 0.0059.
Values may be sent and summed in bfloat16 or wider, within the bound.
A program may use at most 64 MiB of HBM per device.

```python
import math
import jax
import jax.numpy as jnp
from jax import lax

D = 8192
HEADS = 64
HEAD_DIM = 128
ROWS = 128
SPAN = 4
LENGTH = 4096
N_MP = 16


def draw_queries(key, part):
    key = jax.random.fold_in(key, 11)
    sampled = 1.5 * jnp.clip(jax.random.normal(key, (LENGTH, D), jnp.float32), -4.0, 4.0)
    return sampled.astype(jnp.bfloat16)


def draw_key_rows(key, part):
    key = jax.random.fold_in(key, 13)
    sampled = 1.5 * jnp.clip(jax.random.normal(key, (LENGTH, D), jnp.float32), -4.0, 4.0)
    return sampled.astype(jnp.bfloat16)


def draw_filter_taps(key, part):
    key = jax.random.fold_in(key, 5)
    subkeys = jax.random.split(key, 4)
    slow_share = 0.5
    slow_mask = jax.random.uniform(subkeys[0], (D,), jnp.float32) < slow_share
    fraction = jax.random.uniform(subkeys[1], (D,), jnp.float32)
    low_slow = math.log(0.25 / LENGTH)
    high_slow = math.log(2.3 / LENGTH)
    high_fast = math.log(1.0 / 30.0)
    decay_rate = jnp.exp(jnp.where(slow_mask, low_slow + fraction * (high_slow - low_slow), high_slow + fraction * (high_fast - high_slow)))
    position = jnp.arange(LENGTH, dtype=jnp.float32)
    normalizer = jnp.sqrt(jnp.expm1(-2.0 * decay_rate) / jnp.expm1(-2.0 * decay_rate * LENGTH))
    envelope = jnp.exp(-decay_rate[None, :] * position[:, None]) * normalizer[None, :]
    far_share = jax.random.uniform(subkeys[3], (D,), jnp.float32, 0.1, 0.2)
    envelope = jnp.sqrt(1.0 - far_share)[None, :] * envelope + jnp.sqrt(far_share / LENGTH)[None, :]
    roughness = jnp.clip(jax.random.normal(subkeys[2], (LENGTH, D), jnp.float32), -3.5, 3.5)
    return (envelope * roughness).astype(jnp.float32)


def draw_gate_out(key, part):
    key = jax.random.fold_in(key, 7)
    column = jnp.arange(D, dtype=jnp.float32) / D
    column_scale = jnp.sqrt(1.0 + 2.0 * column)
    sampled = jnp.clip(jax.random.normal(key, (LENGTH, D), jnp.float32), -4.0, 4.0)
    return (sampled * column_scale[None, :]).astype(jnp.bfloat16)


def block_levels(stream_key, shape, cuts, smallest, high):
    factor_of = 1.0
    for axis_at, blocks in cuts:
        draws = jax.random.uniform(jax.random.fold_in(jax.random.fold_in(stream_key, 6), axis_at), (blocks,), jnp.float32, smallest / len(cuts), high / len(cuts))
        factor_of = factor_of * jnp.repeat(jnp.exp(draws), shape[axis_at] // blocks).reshape((-1,) + (1,) * (len(shape) - 1 - axis_at))
    return factor_of


def gaussian(stream_key, dims, scale, reach, shards=(), kind=jnp.bfloat16):
    gain = block_levels(stream_key, dims, shards, -0.22, 0.18) if shards else 1.0
    result = jax.random.normal(stream_key, dims, jnp.float32) * scale * gain
    return jnp.minimum(jnp.maximum(result, -reach), reach).astype(kind)


def setup_inputs(seed: int = 0) -> dict:
    keys = jax.random.split(jax.random.key(seed), 8)
    gate_in = gaussian(keys[0], (LENGTH, D), 1.0, 6.0, ((0, 32), (1, 16)))
    value_in = gaussian(keys[1], (LENGTH, D), 1.0, 6.0, ((0, 32), (1, 16)))
    gate_out = draw_gate_out(jax.random.fold_in(keys[7], 71), 0)
    filter_taps = draw_filter_taps(jax.random.fold_in(keys[7], 71), 0)
    skip_gain = jnp.clip(1.0 + 0.18 * jax.random.normal(keys[4], (D,), jnp.float32), 0.1, 1.9)
    queries = draw_queries(jax.random.fold_in(keys[7], 71), 0)
    key_rows = draw_key_rows(jax.random.fold_in(keys[7], 71), 0)
    return dict(gate_in=gate_in, value_in=value_in, gate_out=gate_out, filter_taps=filter_taps, skip_gain=skip_gain, queries=queries, key_rows=key_rows)


def causal_block(operands):
    signal, filter_taps = operands
    span_len = 2 * signal.shape[0]
    spectrum = jnp.fft.rfft(signal, n=span_len, axis=0) * jnp.fft.rfft(filter_taps, n=span_len, axis=0)
    return jnp.fft.irfft(spectrum, n=span_len, axis=0)[:signal.shape[0]]

def head_attention(triple):
    query_h, key_h, value_h = triple
    scores = jnp.dot(query_h, key_h.T, preferred_element_type=jnp.float32) * (1.0 / math.sqrt(HEAD_DIM))
    positions = jnp.arange(LENGTH, dtype=jnp.int32)
    allowed = (positions[None, :] <= positions[:, None]) & (positions[None, :] > positions[:, None] - SPAN * ROWS)
    scores = jnp.where(allowed, scores, -1e+30)
    row_top = lax.optimization_barrier(jnp.max(scores, axis=1, keepdims=True))
    weights = jnp.exp(scores - row_top)
    denominator = lax.optimization_barrier(jnp.sum(weights, axis=1, keepdims=True))
    summed = jnp.dot(weights.astype(jnp.bfloat16), value_h, preferred_element_type=jnp.float32)
    return summed / denominator

def reference(gate_in, value_in, gate_out, filter_taps, skip_gain, queries, key_rows):
    signal = gate_in.astype(jnp.float32) * value_in.astype(jnp.float32)
    groups = N_MP
    group_width = D // groups

    def by_group(matrix):
        return matrix.reshape(LENGTH, groups, group_width).transpose(1, 0, 2)
    convolved = lax.map(causal_block, (by_group(signal), by_group(filter_taps)))
    convolved = convolved.transpose(1, 0, 2).reshape(LENGTH, D)
    mixer_full = gate_out.astype(jnp.float32) * (convolved + skip_gain[None, :] * signal)
    mixer_out = mixer_full.astype(jnp.bfloat16)
    widened = mixer_out.astype(jnp.float32)
    row_scale = lax.rsqrt(lax.optimization_barrier(jnp.mean(widened * widened, axis=1, keepdims=True)) + 1e-06)
    values = (widened * row_scale).astype(jnp.bfloat16)

    def by_head(matrix):
        return matrix.reshape(LENGTH, HEADS, HEAD_DIM).transpose(1, 0, 2)
    attended = lax.map(head_attention, (by_head(queries), by_head(key_rows), by_head(values)))
    attended = attended.transpose(1, 0, 2).reshape(LENGTH, D).astype(jnp.bfloat16)
    return (mixer_out, attended)
```

```python
import functools
import math

import jax
import jax.numpy as jnp
import ml_dtypes
import numpy as np
from jax import lax
from jax.experimental import pallas as pl
from jax.experimental.pallas import tpu as pltpu
from jax.sharding import PartitionSpec as P

HEAD = 128
ROWS = 128
SPAN = 4
NX = 4
MESH = pl.DeviceIdType.MESH
F32 = jnp.float32
BF16 = jnp.bfloat16


def split(table):
    high = table.astype(np.float32).astype(ml_dtypes.bfloat16)
    low = (table - high.astype(np.float64)).astype(np.float32).astype(ml_dtypes.bfloat16)
    return high, low


def tables(blocks):
    length = blocks * ROWS
    n1 = np.arange(blocks)[None, :]
    k1 = np.arange(blocks)[:, None] + 0.25
    n2 = np.arange(ROWS)[None, :]
    first = np.exp(-2j * np.pi * n1 * k1 / blocks)
    twist = np.exp(-2j * np.pi * n2 * k1 / length)
    second = np.exp(-2j * np.pi * n2 * n2.T / ROWS)
    first_high, first_low = split(np.concatenate([first.real, first.imag], 0))
    first_cat = np.concatenate([first_high, first_low], 1)
    wide = np.block([[second.real, second.imag], [-second.imag, second.real]])
    wide_high, wide_low = split(wide)
    last_high, last_low = split(np.concatenate([first.real, first.imag], 0).T / length)
    last_cat = np.concatenate([last_high, last_low, last_high], 1)
    twists = np.stack([twist.real, twist.imag]).astype(np.float32)
    return first_cat, twists, wide_high, wide_low, last_cat


def halves(value):
    high = value.astype(BF16)
    return high, (value - high.astype(F32)).astype(BF16)


def kernel(
    blocks, n_mp, model,
    gate_ref, value_ref, out_gate_ref, taps_ref, query_ref, key_ref, skip_ref,
    first_ref, twist_ref, wide_high_ref, wide_low_ref, last_ref,
    mixer_ref, attended_ref,
    send_taps, send_signal, send_gate, recv_taps, recv_signal, work, spectrum,
    gate_head, query_head, key_head, back_send, back_recv, value_head, probs, denoms,
    power_mp, power_x, mixer_send, attended_send,
    send_sems, recv_sems,
):
    me = lax.axis_index("ctx")
    mp = lax.axis_index("mp")
    x, y = lax.rem(me, NX), lax.div(me, NX)
    n_y = blocks // NX
    width = NX * HEAD // blocks

    barrier = pltpu.get_barrier_semaphore()

    def greet_ctx(k, carry):
        pl.semaphore_signal(barrier, inc=1, device_id={"ctx": lax.rem(me + k, blocks)}, device_id_type=MESH)
        return carry

    def greet_mp(k, carry):
        pl.semaphore_signal(barrier, inc=1, device_id={"mp": lax.rem(mp + k, n_mp)}, device_id_type=MESH)
        return carry

    lax.fori_loop(1, blocks, greet_ctx, 0)
    lax.fori_loop(1, n_mp, greet_mp, 0)

    def send(src, dst, which, target):
        pltpu.make_async_remote_copy(
            src_ref=src, dst_ref=dst, send_sem=send_sems.at[which], recv_sem=recv_sems.at[which],
            device_id=target, device_id_type=MESH,
        ).start()

    def received(ref, which):
        pltpu.make_async_copy(ref, ref, recv_sems.at[which]).wait()

    def sent(ref, which):
        pltpu.make_async_copy(ref, ref, send_sems.at[which]).wait()

    def group(d):
        return pl.ds(pl.multiple_of(lax.rem(d, NX) * HEAD + lax.div(d, NX) * width, width), width)

    mine = pl.ds(pl.multiple_of(me * width, width), width)
    my_lanes = pl.ds(pl.multiple_of(x * HEAD, HEAD), HEAD)

    send_taps[...] = taps_ref[...].T.astype(BF16)
    send_signal[...] = (gate_ref[...].astype(F32) * value_ref[...].astype(F32)).T.astype(BF16)
    pl.semaphore_wait(barrier, blocks - 1 + n_mp - 1)

    def spread(which, src, dst):
        def step(k, carry):
            d = lax.rem(me + k, blocks)
            send(src.at[group(d)], dst.at[mine], which, {"ctx": d})
            return carry
        lax.fori_loop(1, blocks, step, 0)
        dst[mine] = src[group(me)]

    spread(0, send_taps, recv_taps)
    spread(1, send_signal, recv_signal)

    send_gate[...] = out_gate_ref[...].astype(F32).T.astype(BF16)
    own_rows = pl.ds(pl.multiple_of(SPAN * ROWS + x * ROWS, ROWS), ROWS)
    for k in range(1, NX):
        px = lax.rem(x + k, NX)
        target = {"ctx": y * NX + px}
        lanes = pl.ds(pl.multiple_of(px * HEAD, HEAD), HEAD)
        send(key_ref.at[:, lanes], key_head.at[own_rows], 2, target)
        send(query_ref.at[:, lanes], query_head.at[x], 3, target)
        send(send_gate.at[lanes], gate_head.at[x], 4, target)
    key_head[own_rows] = key_ref[:, my_lanes]
    query_head[x] = query_ref[:, my_lanes]
    gate_head[x] = send_gate[my_lanes]

    next_row = lax.rem(me + NX, blocks)
    received(key_head.at[pl.ds(0, (NX - 1) * ROWS)], 2)
    send(key_head.at[pl.ds(SPAN * ROWS, SPAN * ROWS)], key_head.at[pl.ds(0, SPAN * ROWS)], 5, {"ctx": next_row})

    twist_real, twist_imag = twist_ref[0], twist_ref[1]

    def times_wide(value, contract):
        high, low = halves(value)
        dims = (((1,), (contract,)), ((), ()))

        def dot(a, b):
            return lax.dot_general(a, b, dims, preferred_element_type=F32)

        return dot(high, wide_high_ref[...]) + dot(low, wide_high_ref[...]) + dot(high, wide_low_ref[...])

    def lane_tile(value, c):
        return value[:, c * ROWS:(c + 1) * ROWS]

    def forward(recv):
        work[...] = recv[...].astype(F32)
        panel = jnp.concatenate([work[pl.ds(c, blocks, stride=width), :] for c in range(width)], 1).astype(BF16)
        panel = jnp.concatenate([panel, panel], 0)
        bins = jnp.dot(first_ref[...], panel, preferred_element_type=F32)
        real, imag = bins[:blocks], bins[blocks:]
        rows = []
        for c in range(width):
            a, b = lane_tile(real, c), lane_tile(imag, c)
            rows.append(jnp.concatenate([a * twist_real - b * twist_imag, a * twist_imag + b * twist_real], 1))
        return times_wide(jnp.concatenate(rows, 0), 0)

    taps_rows = pl.ds(0, (blocks - 1) * width)
    received(recv_taps.at[taps_rows], 0)
    spectrum[...] = forward(recv_taps)
    skip_at = x * HEAD + y * width
    for c in range(width):
        rows = pl.ds(c * blocks, blocks)
        spectrum[rows, pl.ds(0, ROWS)] = spectrum[rows, pl.ds(0, ROWS)] + skip_ref[skip_at + c]
    received(recv_signal.at[taps_rows], 1)
    bins = forward(recv_signal)
    a, b = bins[:, :ROWS], bins[:, ROWS:]
    c, d = spectrum[:, pl.ds(0, ROWS)], spectrum[:, pl.ds(ROWS, ROWS)]
    back = times_wide(jnp.concatenate([a * c - b * d, a * d + b * c], 1), 1)
    columns = []
    for c in range(width):
        part = back[c * blocks:(c + 1) * blocks]
        a, b = part[:, :ROWS], part[:, ROWS:]
        columns.append(jnp.concatenate([a * twist_real + b * twist_imag, b * twist_real - a * twist_imag], 0))
    high, low = halves(jnp.concatenate(columns, 1))
    convolved = jnp.dot(last_ref[...], jnp.concatenate([high, high, low], 0), preferred_element_type=F32)
    for c in range(width):
        work[pl.ds(c, blocks, stride=width), :] = lane_tile(convolved, c)
    back_send[...] = work[...].astype(BF16).reshape(blocks, width, ROWS)
    for k in range(1, n_y):
        py = lax.rem(y + k, n_y)
        send(back_send.at[pl.ds(py * NX, NX)], back_recv.at[:, y], 6, {"ctx": py * NX + x})
    back_recv[:, y] = back_send[pl.ds(y * NX, NX)]

    received(query_head.at[pl.ds(0, NX - 1)], 3)
    received(key_head.at[pl.ds(0, SPAN * ROWS)], 5)
    reach = (SPAN + 1) * ROWS
    for j in range(NX):
        scores = lax.dot_general(
            key_head[pl.ds(j * ROWS, reach)], query_head[j], (((1,), (1,)), ((), ())), preferred_element_type=F32
        ) * (1.0 / math.sqrt(HEAD))
        key_at = lax.broadcasted_iota(jnp.int32, (reach, ROWS), 0)
        query_at = lax.broadcasted_iota(jnp.int32, (reach, ROWS), 1)
        first_key = jnp.where(y > 0, 0, SPAN * ROWS - j * ROWS)
        allowed = (key_at > query_at) & (key_at <= query_at + SPAN * ROWS) & (key_at >= first_key)
        scores = jnp.where(allowed, scores, -1e30)
        weights = jnp.exp(scores - jnp.max(scores, 0, keepdims=True))
        denoms[j] = jnp.broadcast_to(jnp.sum(weights, 0, keepdims=True), (8, ROWS))
        probs[j] = weights.astype(BF16)

    received(gate_head.at[pl.ds(0, NX - 1)], 4)
    received(back_send.at[pl.ds(0, (n_y - 1) * NX)], 6)
    gated = gate_head[...].astype(F32) * back_recv[...].reshape(NX, HEAD, ROWS).astype(F32)
    mixed = gated.astype(BF16)
    value_head[pl.ds(NX, NX)] = mixed
    send(value_head.at[pl.ds(NX, NX)], value_head.at[pl.ds(0, NX)], 7, {"ctx": next_row})
    widened = mixed.astype(F32)
    power = jnp.sum(widened * widened, 1)
    power_mp[mp] = jnp.concatenate([power, jnp.zeros_like(power)], 0)

    def share_power(k, carry):
        send(power_mp.at[mp], power_mp.at[mp], 8, {"mp": lax.rem(mp + k, n_mp)})
        return carry

    lax.fori_loop(1, n_mp, share_power, 0)

    for j in range(NX):
        mixer_send[j] = widened[j].T.astype(BF16)
    for k in range(1, NX):
        px = lax.rem(x + k, NX)
        send(mixer_send.at[px], mixer_ref.at[:, my_lanes], 9, {"ctx": y * NX + px})
    mixer_ref[:, my_lanes] = mixer_send[x]

    received(power_mp.at[pl.ds(0, n_mp - 1)], 8)
    power_x[NX + x] = jnp.sum(power_mp[...], 0)
    next_y = lax.rem(y + 1, n_y)
    for k in range(NX):
        px = lax.rem(x + k, NX)
        if k:
            send(power_x.at[NX + x], power_x.at[NX + x], 10, {"ctx": y * NX + px})
        send(power_x.at[NX + x], power_x.at[x], 11, {"ctx": next_y * NX + px})
    received(power_x.at[pl.ds(0, NX - 1)], 10)
    received(power_x.at[pl.ds(0, NX)], 11)
    received(value_head.at[pl.ds(0, NX)], 7)
    values = []
    for half in range(2):
        total = power_x[half * NX]
        for k in range(1, NX):
            total = total + power_x[half * NX + k]
        scale = lax.rsqrt(total * (1.0 / model) + 1e-06)
        for j in range(NX):
            values.append((value_head[half * NX + j].astype(F32) * scale[j:j + 1]).astype(BF16))
    for j in range(NX):
        summed = jnp.dot(jnp.concatenate(values[j:j + SPAN + 1], 1), probs[j], preferred_element_type=F32)
        attended_send[j] = (summed / denoms[j][0:1]).T.astype(BF16)
    for k in range(1, NX):
        px = lax.rem(x + k, NX)
        send(attended_send.at[px], attended_ref.at[:, my_lanes], 12, {"ctx": y * NX + px})
    attended_ref[:, my_lanes] = attended_send[x]

    sent(recv_taps.at[taps_rows], 0)
    sent(recv_signal.at[taps_rows], 1)
    sent(key_head.at[pl.ds(0, (NX - 1) * ROWS)], 2)
    sent(query_head.at[pl.ds(0, NX - 1)], 3)
    sent(gate_head.at[pl.ds(0, NX - 1)], 4)
    sent(key_head.at[pl.ds(0, SPAN * ROWS)], 5)
    sent(back_send.at[pl.ds(0, (n_y - 1) * NX)], 6)
    sent(value_head.at[pl.ds(0, NX)], 7)
    sent(power_mp.at[pl.ds(0, n_mp - 1)], 8)
    sent(mixer_send.at[pl.ds(0, NX - 1)], 9)
    sent(power_x.at[pl.ds(0, NX - 1)], 10)
    sent(power_x.at[pl.ds(0, NX)], 11)
    sent(attended_send.at[pl.ds(0, NX - 1)], 12)
    received(mixer_send.at[pl.ds(0, NX - 1)], 9)
    received(attended_send.at[pl.ds(0, NX - 1)], 12)


def solution(mesh):
    blocks, n_mp = mesh.shape["ctx"], mesh.shape["mp"]
    constants = tables(blocks)

    def local(gate_in, value_in, gate_out, filter_taps, skip_gain, queries, key_rows):
        rows, lanes = gate_in.shape
        width = lanes // blocks
        n_y = blocks // NX
        vmem = pl.BlockSpec(memory_space=pltpu.VMEM)
        square = (NX, ROWS, HEAD)
        return pl.pallas_call(
            functools.partial(kernel, blocks, n_mp, n_mp * lanes),
            out_shape=(jax.ShapeDtypeStruct((rows, lanes), BF16),) * 2,
            in_specs=[vmem] * 6 + [pl.BlockSpec(memory_space=pltpu.SMEM)] + [vmem] * 5,
            out_specs=(vmem, vmem),
            scratch_shapes=[
                pltpu.VMEM((lanes, ROWS), BF16),
                pltpu.VMEM((lanes, ROWS), BF16),
                pltpu.VMEM((lanes, ROWS), BF16),
                pltpu.VMEM((lanes, ROWS), BF16),
                pltpu.VMEM((lanes, ROWS), BF16),
                pltpu.VMEM((lanes, ROWS), F32),
                pltpu.VMEM((lanes, 2 * ROWS), F32),
                pltpu.VMEM(square, BF16),
                pltpu.VMEM(square, BF16),
                pltpu.VMEM((2 * SPAN * ROWS, HEAD), BF16),
                pltpu.VMEM((blocks, width, ROWS), BF16),
                pltpu.VMEM((NX, n_y, width, ROWS), BF16),
                pltpu.VMEM((2 * NX, HEAD, ROWS), BF16),
                pltpu.VMEM((NX, (SPAN + 1) * ROWS, ROWS), BF16),
                pltpu.VMEM((NX, 8, ROWS), F32),
                pltpu.VMEM((n_mp, 8, ROWS), F32),
                pltpu.VMEM((2 * NX, 8, ROWS), F32),
                pltpu.VMEM(square, BF16),
                pltpu.VMEM(square, BF16),
                pltpu.SemaphoreType.DMA((13,)),
                pltpu.SemaphoreType.DMA((13,)),
            ],
            compiler_params=pltpu.CompilerParams(
                collective_id=0, has_side_effects=True, vmem_limit_bytes=48 * 2**20
            ),
            cost_estimate=pl.CostEstimate(flops=2 * 10**9, bytes_accessed=2 * 10**6, transcendentals=4 * 10**5),
        )(gate_in, value_in, gate_out, filter_taps, queries, key_rows, skip_gain, *constants)

    return jax.shard_map(
        local,
        mesh=mesh,
        in_specs=(P("ctx", "mp"),) * 4 + (P("mp"),) + (P("ctx", "mp"),) * 2,
        out_specs=(P("ctx", "mp"), P("ctx", "mp")),
        check_vma=False,
    )
```

```python
import functools
import math

import jax
import jax.numpy as jnp
import ml_dtypes
import numpy as np
from jax import lax
from jax.experimental import pallas as pl
from jax.experimental.pallas import tpu as pltpu
from jax.sharding import PartitionSpec as P

HEAD = 128
ROWS = 128
SPAN = 4
NX = 4
MESH = pl.DeviceIdType.MESH
F32 = jnp.float32
BF16 = jnp.bfloat16


def split(table):
    high = table.astype(np.float32).astype(ml_dtypes.bfloat16)
    low = (table - high.astype(np.float64)).astype(np.float32).astype(ml_dtypes.bfloat16)
    return high, low


def tables(blocks):
    length = blocks * ROWS
    n1 = np.arange(blocks)[None, :]
    k1 = np.arange(blocks)[:, None] + 0.25
    n2 = np.arange(ROWS)[None, :]
    first = np.exp(-2j * np.pi * n1 * k1 / blocks)
    twist = np.exp(-2j * np.pi * n2 * k1 / length)
    second = np.exp(-2j * np.pi * n2 * n2.T / ROWS)
    first_high, first_low = split(np.concatenate([first.real, first.imag], 0))
    first_cat = np.concatenate([first_high, first_low], 1)
    wide = np.block([[second.real, second.imag], [-second.imag, second.real]])
    wide_high, wide_low = split(wide)
    last_high, last_low = split(np.concatenate([first.real, first.imag], 0).T / length)
    last_cat = np.concatenate([last_high, last_low, last_high], 1)
    twists = np.stack([twist.real, twist.imag]).astype(np.float32)
    return first_cat, twists, wide_high, wide_low, last_cat


def halves(value):
    high = value.astype(BF16)
    return high, (value - high.astype(F32)).astype(BF16)


def kernel(
    blocks, n_mp, model,
    gate_hbm, value_hbm, out_gate_hbm, taps_hbm, query_hbm, key_hbm, skip_hbm,
    first_hbm, twist_hbm, wide_high_hbm, wide_low_hbm, last_hbm,
    mixer_hbm, attended_hbm,
    gate_ref, value_ref, out_gate_ref, taps_ref, skip_ref,
    first_ref, twist_ref, wide_high_ref, wide_low_ref, last_ref,
    send_taps, send_signal, send_gate, recv_taps, recv_signal, work, spectrum,
    gate_head, query_head, key_head, back_send, back_recv, value_head, probs, denoms,
    power_mp, power_x, mixer_send, attended_send,
    local_sems, send_sems, recv_sems,
):
    me = lax.axis_index("ctx")
    mp = lax.axis_index("mp")
    x, y = lax.rem(me, NX), lax.div(me, NX)
    n_y = blocks // NX
    width = NX * HEAD // blocks

    def fetch(src, dst, which):
        copy = pltpu.make_async_copy(src, dst, local_sems.at[which])
        copy.start()
        return copy

    loads = [
        fetch(src, dst, which)
        for which, (src, dst) in enumerate([
            (taps_hbm, taps_ref), (gate_hbm, gate_ref), (value_hbm, value_ref), (out_gate_hbm, out_gate_ref),
            (first_hbm, first_ref), (twist_hbm, twist_ref), (wide_high_hbm, wide_high_ref),
            (wide_low_hbm, wide_low_ref), (last_hbm, last_ref), (skip_hbm, skip_ref),
        ])
    ]
    barrier = pltpu.get_barrier_semaphore()

    def greet_ctx(k, carry):
        pl.semaphore_signal(barrier, inc=1, device_id={"ctx": lax.rem(me + k, blocks)}, device_id_type=MESH)
        return carry

    def greet_mp(k, carry):
        pl.semaphore_signal(barrier, inc=1, device_id={"mp": lax.rem(mp + k, n_mp)}, device_id_type=MESH)
        return carry

    lax.fori_loop(1, blocks, greet_ctx, 0)
    lax.fori_loop(1, n_mp, greet_mp, 0)

    def send(src, dst, which, target):
        pltpu.make_async_remote_copy(
            src_ref=src, dst_ref=dst, send_sem=send_sems.at[which], recv_sem=recv_sems.at[which],
            device_id=target, device_id_type=MESH,
        ).start()

    def received(ref, which):
        pltpu.make_async_copy(ref, ref, recv_sems.at[which]).wait()

    def sent(ref, which):
        pltpu.make_async_copy(ref, ref, send_sems.at[which]).wait()

    def group(d):
        return pl.ds(pl.multiple_of(lax.rem(d, NX) * HEAD + lax.div(d, NX) * width, width), width)

    mine = pl.ds(pl.multiple_of(me * width, width), width)
    my_lanes = pl.ds(pl.multiple_of(x * HEAD, HEAD), HEAD)

    loads[0].wait()
    send_taps[...] = taps_ref[...].T.astype(BF16)
    loads[1].wait()
    loads[2].wait()
    send_signal[...] = (gate_ref[...].astype(F32) * value_ref[...].astype(F32)).T.astype(BF16)
    pl.semaphore_wait(barrier, blocks - 1 + n_mp - 1)

    def spread(which, src, dst):
        def step(k, carry):
            d = lax.rem(me + k, blocks)
            send(src.at[group(d)], dst.at[mine], which, {"ctx": d})
            return carry
        lax.fori_loop(1, blocks, step, 0)
        dst[mine] = src[group(me)]

    spread(0, send_taps, recv_taps)
    spread(1, send_signal, recv_signal)

    loads[3].wait()
    send_gate[...] = out_gate_ref[...].astype(F32).T.astype(BF16)
    own_rows = pl.ds(pl.multiple_of(SPAN * ROWS + x * ROWS, ROWS), ROWS)
    for k in range(1, NX):
        px = lax.rem(x + k, NX)
        target = {"ctx": y * NX + px}
        lanes = pl.ds(pl.multiple_of(px * HEAD, HEAD), HEAD)
        send(key_hbm.at[:, lanes], key_head.at[own_rows], 2, target)
        send(query_hbm.at[:, lanes], query_head.at[x], 3, target)
        send(send_gate.at[lanes], gate_head.at[x], 4, target)
    own_key = fetch(key_hbm.at[:, my_lanes], key_head.at[own_rows], 10)
    own_query = fetch(query_hbm.at[:, my_lanes], query_head.at[x], 11)
    gate_head[x] = send_gate[my_lanes]

    next_row = lax.rem(me + NX, blocks)
    own_key.wait()
    received(key_head.at[pl.ds(0, (NX - 1) * ROWS)], 2)
    send(key_head.at[pl.ds(SPAN * ROWS, SPAN * ROWS)], key_head.at[pl.ds(0, SPAN * ROWS)], 5, {"ctx": next_row})

    for load in loads[4:]:
        load.wait()
    twist_real, twist_imag = twist_ref[0], twist_ref[1]

    def times_wide(value, contract):
        high, low = halves(value)
        dims = (((1,), (contract,)), ((), ()))

        def dot(a, b):
            return lax.dot_general(a, b, dims, preferred_element_type=F32)

        return dot(high, wide_high_ref[...]) + dot(low, wide_high_ref[...]) + dot(high, wide_low_ref[...])

    def lane_tile(value, c):
        return value[:, c * ROWS:(c + 1) * ROWS]

    def forward(recv):
        work[...] = recv[...].astype(F32)
        panel = jnp.concatenate([work[pl.ds(c, blocks, stride=width), :] for c in range(width)], 1).astype(BF16)
        panel = jnp.concatenate([panel, panel], 0)
        bins = jnp.dot(first_ref[...], panel, preferred_element_type=F32)
        real, imag = bins[:blocks], bins[blocks:]
        rows = []
        for c in range(width):
            a, b = lane_tile(real, c), lane_tile(imag, c)
            rows.append(jnp.concatenate([a * twist_real - b * twist_imag, a * twist_imag + b * twist_real], 1))
        return times_wide(jnp.concatenate(rows, 0), 0)

    taps_rows = pl.ds(0, (blocks - 1) * width)
    received(recv_taps.at[taps_rows], 0)
    spectrum[...] = forward(recv_taps)
    skip_at = x * HEAD + y * width
    for c in range(width):
        rows = pl.ds(c * blocks, blocks)
        spectrum[rows, pl.ds(0, ROWS)] = spectrum[rows, pl.ds(0, ROWS)] + skip_ref[skip_at + c]
    received(recv_signal.at[taps_rows], 1)
    bins = forward(recv_signal)
    a, b = bins[:, :ROWS], bins[:, ROWS:]
    c, d = spectrum[:, pl.ds(0, ROWS)], spectrum[:, pl.ds(ROWS, ROWS)]
    back = times_wide(jnp.concatenate([a * c - b * d, a * d + b * c], 1), 1)
    columns = []
    for c in range(width):
        part = back[c * blocks:(c + 1) * blocks]
        a, b = part[:, :ROWS], part[:, ROWS:]
        columns.append(jnp.concatenate([a * twist_real + b * twist_imag, b * twist_real - a * twist_imag], 0))
    high, low = halves(jnp.concatenate(columns, 1))
    convolved = jnp.dot(last_ref[...], jnp.concatenate([high, high, low], 0), preferred_element_type=F32)
    for c in range(width):
        work[pl.ds(c, blocks, stride=width), :] = lane_tile(convolved, c)
    back_send[...] = work[...].astype(BF16).reshape(blocks, width, ROWS)
    for k in range(1, n_y):
        py = lax.rem(y + k, n_y)
        send(back_send.at[pl.ds(py * NX, NX)], back_recv.at[:, y], 6, {"ctx": py * NX + x})
    back_recv[:, y] = back_send[pl.ds(y * NX, NX)]

    own_query.wait()
    received(query_head.at[pl.ds(0, NX - 1)], 3)
    received(key_head.at[pl.ds(0, SPAN * ROWS)], 5)
    reach = (SPAN + 1) * ROWS
    for j in range(NX):
        scores = lax.dot_general(
            key_head[pl.ds(j * ROWS, reach)], query_head[j], (((1,), (1,)), ((), ())), preferred_element_type=F32
        ) * (1.0 / math.sqrt(HEAD))
        key_at = lax.broadcasted_iota(jnp.int32, (reach, ROWS), 0)
        query_at = lax.broadcasted_iota(jnp.int32, (reach, ROWS), 1)
        first_key = jnp.where(y > 0, 0, SPAN * ROWS - j * ROWS)
        allowed = (key_at > query_at) & (key_at <= query_at + SPAN * ROWS) & (key_at >= first_key)
        scores = jnp.where(allowed, scores, -1e30)
        weights = jnp.exp(scores - jnp.max(scores, 0, keepdims=True))
        denoms[j] = jnp.broadcast_to(jnp.sum(weights, 0, keepdims=True), (8, ROWS))
        probs[j] = weights.astype(BF16)

    received(gate_head.at[pl.ds(0, NX - 1)], 4)
    received(back_send.at[pl.ds(0, (n_y - 1) * NX)], 6)
    gated = gate_head[...].astype(F32) * back_recv[...].reshape(NX, HEAD, ROWS).astype(F32)
    mixed = gated.astype(BF16)
    value_head[pl.ds(NX, NX)] = mixed
    send(value_head.at[pl.ds(NX, NX)], value_head.at[pl.ds(0, NX)], 7, {"ctx": next_row})
    widened = mixed.astype(F32)
    power = jnp.sum(widened * widened, 1)
    power_mp[mp] = jnp.concatenate([power, jnp.zeros_like(power)], 0)

    def share_power(k, carry):
        send(power_mp.at[mp], power_mp.at[mp], 8, {"mp": lax.rem(mp + k, n_mp)})
        return carry

    lax.fori_loop(1, n_mp, share_power, 0)

    for j in range(NX):
        mixer_send[j] = widened[j].T.astype(BF16)
    for k in range(1, NX):
        px = lax.rem(x + k, NX)
        send(mixer_send.at[px], mixer_hbm.at[:, my_lanes], 9, {"ctx": y * NX + px})
    own_mixer = fetch(mixer_send.at[x], mixer_hbm.at[:, my_lanes], 12)

    received(power_mp.at[pl.ds(0, n_mp - 1)], 8)
    power_x[NX + x] = jnp.sum(power_mp[...], 0)
    next_y = lax.rem(y + 1, n_y)
    for k in range(NX):
        px = lax.rem(x + k, NX)
        if k:
            send(power_x.at[NX + x], power_x.at[NX + x], 10, {"ctx": y * NX + px})
        send(power_x.at[NX + x], power_x.at[x], 11, {"ctx": next_y * NX + px})
    received(power_x.at[pl.ds(0, NX - 1)], 10)
    received(power_x.at[pl.ds(0, NX)], 11)
    received(value_head.at[pl.ds(0, NX)], 7)
    values = []
    for half in range(2):
        total = power_x[half * NX]
        for k in range(1, NX):
            total = total + power_x[half * NX + k]
        scale = lax.rsqrt(total * (1.0 / model) + 1e-06)
        for j in range(NX):
            values.append((value_head[half * NX + j].astype(F32) * scale[j:j + 1]).astype(BF16))
    for j in range(NX):
        summed = jnp.dot(jnp.concatenate(values[j:j + SPAN + 1], 1), probs[j], preferred_element_type=F32)
        attended_send[j] = (summed / denoms[j][0:1]).T.astype(BF16)
    for k in range(1, NX):
        px = lax.rem(x + k, NX)
        send(attended_send.at[px], attended_hbm.at[:, my_lanes], 12, {"ctx": y * NX + px})
    own_attended = fetch(attended_send.at[x], attended_hbm.at[:, my_lanes], 13)
    own_mixer.wait()
    own_attended.wait()

    sent(recv_taps.at[taps_rows], 0)
    sent(recv_signal.at[taps_rows], 1)
    sent(key_head.at[pl.ds(0, (NX - 1) * ROWS)], 2)
    sent(query_head.at[pl.ds(0, NX - 1)], 3)
    sent(gate_head.at[pl.ds(0, NX - 1)], 4)
    sent(key_head.at[pl.ds(0, SPAN * ROWS)], 5)
    sent(back_send.at[pl.ds(0, (n_y - 1) * NX)], 6)
    sent(value_head.at[pl.ds(0, NX)], 7)
    sent(power_mp.at[pl.ds(0, n_mp - 1)], 8)
    sent(mixer_send.at[pl.ds(0, NX - 1)], 9)
    sent(power_x.at[pl.ds(0, NX - 1)], 10)
    sent(power_x.at[pl.ds(0, NX)], 11)
    sent(attended_send.at[pl.ds(0, NX - 1)], 12)
    received(mixer_send.at[pl.ds(0, NX - 1)], 9)
    received(attended_send.at[pl.ds(0, NX - 1)], 12)


def solution(mesh):
    blocks, n_mp = mesh.shape["ctx"], mesh.shape["mp"]
    constants = tables(blocks)

    def local(gate_in, value_in, gate_out, filter_taps, skip_gain, queries, key_rows):
        rows, lanes = gate_in.shape
        width = lanes // blocks
        n_y = blocks // NX
        hbm = pl.BlockSpec(memory_space=pltpu.HBM)
        square = (NX, ROWS, HEAD)
        return pl.pallas_call(
            functools.partial(kernel, blocks, n_mp, n_mp * lanes),
            out_shape=(jax.ShapeDtypeStruct((rows, lanes), BF16),) * 2,
            in_specs=[hbm] * 12,
            out_specs=(hbm, hbm),
            scratch_shapes=[
                pltpu.VMEM((rows, lanes), BF16),
                pltpu.VMEM((rows, lanes), BF16),
                pltpu.VMEM((rows, lanes), BF16),
                pltpu.VMEM((rows, lanes), F32),
                pltpu.SMEM((lanes,), F32),
                *(pltpu.VMEM(c.shape, c.dtype) for c in constants),
                pltpu.VMEM((lanes, ROWS), BF16),
                pltpu.VMEM((lanes, ROWS), BF16),
                pltpu.VMEM((lanes, ROWS), BF16),
                pltpu.VMEM((lanes, ROWS), BF16),
                pltpu.VMEM((lanes, ROWS), BF16),
                pltpu.VMEM((lanes, ROWS), F32),
                pltpu.VMEM((lanes, 2 * ROWS), F32),
                pltpu.VMEM(square, BF16),
                pltpu.VMEM(square, BF16),
                pltpu.VMEM((2 * SPAN * ROWS, HEAD), BF16),
                pltpu.VMEM((blocks, width, ROWS), BF16),
                pltpu.VMEM((NX, n_y, width, ROWS), BF16),
                pltpu.VMEM((2 * NX, HEAD, ROWS), BF16),
                pltpu.VMEM((NX, (SPAN + 1) * ROWS, ROWS), BF16),
                pltpu.VMEM((NX, 8, ROWS), F32),
                pltpu.VMEM((n_mp, 8, ROWS), F32),
                pltpu.VMEM((2 * NX, 8, ROWS), F32),
                pltpu.VMEM(square, BF16),
                pltpu.VMEM(square, BF16),
                pltpu.SemaphoreType.DMA((14,)),
                pltpu.SemaphoreType.DMA((13,)),
                pltpu.SemaphoreType.DMA((13,)),
            ],
            compiler_params=pltpu.CompilerParams(
                collective_id=0, has_side_effects=True, vmem_limit_bytes=60 * 2**20
            ),
            cost_estimate=pl.CostEstimate(flops=2 * 10**9, bytes_accessed=2 * 10**6, transcendentals=4 * 10**5),
        )(gate_in, value_in, gate_out, filter_taps, queries, key_rows, skip_gain, *constants)

    return jax.shard_map(
        local,
        mesh=mesh,
        in_specs=(P("ctx", "mp"),) * 4 + (P("mp"),) + (P("ctx", "mp"),) * 2,
        out_specs=(P("ctx", "mp"), P("ctx", "mp")),
        check_vma=False,
    )
```

```python
import functools
import math

import jax
import jax.numpy as jnp
import ml_dtypes
import numpy as np
from jax import lax
from jax.experimental import pallas as pl
from jax.experimental.pallas import tpu as pltpu
from jax.sharding import PartitionSpec as P

HEAD = 128
ROWS = 128
SPAN = 4
NX = 4
MESH = pl.DeviceIdType.MESH
F32 = jnp.float32
BF16 = jnp.bfloat16


def split(table):
    high = table.astype(np.float32).astype(ml_dtypes.bfloat16)
    low = (table - high.astype(np.float64)).astype(np.float32).astype(ml_dtypes.bfloat16)
    return high, low


def tables(blocks):
    length = blocks * ROWS
    n1 = np.arange(blocks)[None, :]
    k1 = np.arange(blocks)[:, None] + 0.25
    n2 = np.arange(ROWS)[None, :]
    first = np.exp(-2j * np.pi * n1 * k1 / blocks)
    twist = np.exp(-2j * np.pi * n2 * k1 / length)
    second = np.exp(-2j * np.pi * n2 * n2.T / ROWS)
    first_high, first_low = split(np.concatenate([first.real, first.imag], 0))
    first_cat = np.concatenate([first_high, first_low], 1)
    wide = np.block([[second.real, second.imag], [-second.imag, second.real]])
    wide_high, wide_low = split(wide)
    last_high, last_low = split(np.concatenate([first.real, first.imag], 0).T / length)
    last_cat = np.concatenate([last_high, last_low, last_high], 1)
    twists = np.stack([twist.real, twist.imag]).astype(np.float32)
    return first_cat, twists, wide_high, wide_low, last_cat


def halves(value):
    high = value.astype(BF16)
    return high, (value - high.astype(F32)).astype(BF16)


def kernel(
    blocks, n_mp, model,
    gate_hbm, value_hbm, out_gate_hbm, taps_hbm, query_hbm, key_hbm, skip_hbm,
    first_hbm, twist_hbm, wide_high_hbm, wide_low_hbm, last_hbm,
    mixer_hbm, attended_hbm,
    gate_ref, value_ref, out_gate_ref, taps_ref, query_ref, skip_ref,
    first_ref, twist_ref, wide_high_ref, wide_low_ref, last_ref,
    send_taps, send_signal, send_gate, recv_taps, recv_signal, work, spectrum,
    gate_head, back_send, back_recv, key_all, value_row, value_all, probs, denoms,
    power_x, power_mp, scales, mixer_out, attended_out,
    local_sems, send_sems, recv_sems,
):
    me = lax.axis_index("ctx")
    mp = lax.axis_index("mp")
    x, y = lax.rem(me, NX), lax.div(me, NX)
    n_y = blocks // NX
    width = NX * HEAD // blocks

    def far_first(k, count):
        half = lax.div(k + 1, 2)
        return lax.rem(count // 2 + jnp.where(lax.rem(k, 2) == 1, half, count - half), count)

    def ctx_peer(k):
        px = lax.rem(x + far_first(lax.rem(k, NX), NX), NX)
        py = lax.rem(y + far_first(lax.div(k, NX), n_y), n_y)
        return py * NX + px

    def mp_peer(k):
        return lax.rem(mp + far_first(k, n_mp), n_mp)

    barrier = pltpu.get_barrier_semaphore()

    def greet_ctx(k, carry):
        pl.semaphore_signal(barrier, inc=1, device_id={"ctx": ctx_peer(k)}, device_id_type=MESH)
        return carry

    def greet_mp(k, carry):
        pl.semaphore_signal(barrier, inc=1, device_id={"mp": mp_peer(k)}, device_id_type=MESH)
        return carry

    def fetch(src, dst, which):
        copy = pltpu.make_async_copy(src, dst, local_sems.at[which])
        copy.start()
        return copy

    first_loads = [
        fetch(src, dst, which)
        for which, (src, dst) in enumerate([(taps_hbm, taps_ref), (gate_hbm, gate_ref), (value_hbm, value_ref)])
    ]
    lax.fori_loop(0, blocks - 1, greet_ctx, 0)
    lax.fori_loop(0, n_mp - 1, greet_mp, 0)
    own_rows = pl.ds(SPAN * ROWS, ROWS)
    loads = [
        fetch(src, dst, 3 + which)
        for which, (src, dst) in enumerate([
            (out_gate_hbm, out_gate_ref), (first_hbm, first_ref), (twist_hbm, twist_ref),
            (wide_high_hbm, wide_high_ref), (wide_low_hbm, wide_low_ref), (last_hbm, last_ref), (skip_hbm, skip_ref),
            (query_hbm, query_ref), (key_hbm, key_all.at[own_rows]),
        ])
    ]

    def send(src, dst, which, target, send_which=None):
        pltpu.make_async_remote_copy(
            src_ref=src, dst_ref=dst, send_sem=send_sems.at[which if send_which is None else send_which],
            recv_sem=recv_sems.at[which], device_id=target, device_id_type=MESH,
        ).start()

    def received(ref, which):
        pltpu.make_async_copy(ref, ref, recv_sems.at[which]).wait()

    def sent(ref, which):
        pltpu.make_async_copy(ref, ref, send_sems.at[which]).wait()

    def group(d):
        return pl.ds(pl.multiple_of(lax.rem(d, NX) * HEAD + lax.div(d, NX) * width, width), width)

    mine = pl.ds(pl.multiple_of(me * width, width), width)
    my_lanes = pl.ds(pl.multiple_of(x * HEAD, HEAD), HEAD)

    first_loads[0].wait()
    send_taps[...] = taps_ref[...].T.astype(BF16)
    first_loads[1].wait()
    first_loads[2].wait()
    send_signal[...] = (gate_ref[...].astype(F32) * value_ref[...].astype(F32)).T.astype(BF16)
    pl.semaphore_wait(barrier, blocks - 1 + n_mp - 1)

    def spread(which, src, dst):
        def step(k, carry):
            d = ctx_peer(k)
            send(src.at[group(d)], dst.at[mine], which, {"ctx": d})
            return carry
        lax.fori_loop(0, blocks - 1, step, 0)
        dst[mine] = src[group(me)]

    spread(0, send_taps, recv_taps)
    spread(1, send_signal, recv_signal)

    loads[0].wait()
    send_gate[...] = out_gate_ref[...].astype(F32).T.astype(BF16)
    for k in (2, 1, 3):
        px = lax.rem(x + k, NX)
        lanes = pl.ds(pl.multiple_of(px * HEAD, HEAD), HEAD)
        send(send_gate.at[lanes], gate_head.at[x], 2, {"ctx": y * NX + px})
    gate_head[x] = send_gate[my_lanes]

    for load in loads[1:]:
        load.wait()
    twist_real, twist_imag = twist_ref[0], twist_ref[1]

    def times_wide(value, contract):
        high, low = halves(value)
        dims = (((1,), (contract,)), ((), ()))

        def dot(a, b):
            return lax.dot_general(a, b, dims, preferred_element_type=F32)

        return dot(high, wide_high_ref[...]) + dot(low, wide_high_ref[...]) + dot(high, wide_low_ref[...])

    def lane_tile(value, c):
        return value[:, c * ROWS:(c + 1) * ROWS]

    def forward(recv):
        work[...] = recv[...].astype(F32)
        panel = jnp.concatenate([work[pl.ds(c, blocks, stride=width), :] for c in range(width)], 1).astype(BF16)
        panel = jnp.concatenate([panel, panel], 0)
        bins = jnp.dot(first_ref[...], panel, preferred_element_type=F32)
        real, imag = bins[:blocks], bins[blocks:]
        rows = []
        for c in range(width):
            a, b = lane_tile(real, c), lane_tile(imag, c)
            rows.append(jnp.concatenate([a * twist_real - b * twist_imag, a * twist_imag + b * twist_real], 1))
        return times_wide(jnp.concatenate(rows, 0), 0)

    remote_rows = pl.ds(0, (blocks - 1) * width)
    received(recv_taps.at[remote_rows], 0)
    spectrum[...] = forward(recv_taps)
    skip_at = x * HEAD + y * width
    for c in range(width):
        rows = pl.ds(c * blocks, blocks)
        spectrum[rows, pl.ds(0, ROWS)] = spectrum[rows, pl.ds(0, ROWS)] + skip_ref[skip_at + c]
    received(recv_signal.at[remote_rows], 1)

    next_row = lax.rem(me + NX, blocks)
    own_keys, oldest_keys = key_all.at[own_rows], key_all.at[pl.ds(0, ROWS)]
    send(own_keys, oldest_keys, 3, {"ctx": next_row})
    for px in range(1, NX):
        @pl.when(x < px)
        def _():
            slot = pl.multiple_of((SPAN + x - px) * ROWS, ROWS)
            send(own_keys, key_all.at[pl.ds(slot, ROWS)], 4, {"ctx": y * NX + px})

    bins = forward(recv_signal)
    a, b = bins[:, :ROWS], bins[:, ROWS:]
    c, d = spectrum[:, pl.ds(0, ROWS)], spectrum[:, pl.ds(ROWS, ROWS)]
    back = times_wide(jnp.concatenate([a * c - b * d, a * d + b * c], 1), 1)
    columns = []
    for c in range(width):
        part = back[c * blocks:(c + 1) * blocks]
        a, b = part[:, :ROWS], part[:, ROWS:]
        columns.append(jnp.concatenate([a * twist_real + b * twist_imag, b * twist_real - a * twist_imag], 0))
    high, low = halves(jnp.concatenate(columns, 1))
    convolved = jnp.dot(last_ref[...], jnp.concatenate([high, high, low], 0), preferred_element_type=F32)
    for c in range(width):
        work[pl.ds(c, blocks, stride=width), :] = lane_tile(convolved, c)
    back_send[...] = work[...].astype(BF16).reshape(blocks, width, ROWS)

    def send_back(k, carry):
        py = lax.rem(y + far_first(k, n_y), n_y)
        send(back_send.at[pl.ds(py * NX, NX)], back_recv.at[:, y], 5, {"ctx": py * NX + x})
        return carry

    lax.fori_loop(0, n_y - 1, send_back, 0)
    back_recv[:, y] = back_send[pl.ds(y * NX, NX)]

    received(oldest_keys, 3)
    for px in range(NX - 1):
        @pl.when(x > px)
        def _():
            slot = pl.multiple_of((x - px) * ROWS, ROWS)
            send(oldest_keys, key_all.at[pl.ds(slot, ROWS)], 4, {"ctx": y * NX + px})

    received(gate_head.at[pl.ds(0, NX - 1)], 2)
    received(back_send.at[pl.ds(0, (n_y - 1) * NX)], 5)
    gated = gate_head[...].astype(F32) * back_recv[...].reshape(NX, HEAD, ROWS).astype(F32)
    mixed = gated.astype(BF16)
    value_row[...] = mixed
    widened = mixed.astype(F32)
    power = jnp.sum(widened * widened, 1)
    power_x[NX + x] = jnp.concatenate([power, jnp.zeros_like(power)], 0)
    next_y = lax.rem(y + 1, n_y)
    for k in (2, 1, 3, 0):
        px = lax.rem(x + k, NX)
        send(power_x.at[NX + x], power_x.at[x], 7, {"ctx": next_y * NX + px})
        if k:
            send(power_x.at[NX + x], power_x.at[NX + x], 6, {"ctx": y * NX + px})
    for px in range(NX):
        send(
            value_row.at[pl.ds(px, NX - px)], value_all.at[pl.ds(0, NX - px), x], 8 + x,
            {"ctx": next_y * NX + px}, 8,
        )
    for px in range(NX):
        src, dst = value_row.at[pl.ds(0, px + 1)], value_all.at[pl.ds(SPAN - px, px + 1), x]

        @pl.when(x != px)
        def _():
            send(src, dst, 8 + x, {"ctx": y * NX + px}, 9 + px)

        @pl.when(x == px)
        def _():
            pltpu.make_async_copy(src, dst, recv_sems.at[8 + x]).start()

    received(key_all.at[pl.ds(0, (NX - 1) * ROWS)], 4)
    reach = (SPAN + 1) * ROWS
    key_at = lax.broadcasted_iota(jnp.int32, (reach, ROWS), 0)
    query_at = lax.broadcasted_iota(jnp.int32, (reach, ROWS), 1)
    first_key = jnp.maximum(SPAN - me, 0) * ROWS
    allowed = (key_at > query_at) & (key_at <= query_at + SPAN * ROWS) & (key_at >= first_key)
    for h in range(NX):
        lanes = pl.ds(h * HEAD, HEAD)
        scores = lax.dot_general(
            key_all[:, lanes], query_ref[:, lanes], (((1,), (1,)), ((), ())), preferred_element_type=F32
        ) * (1.0 / math.sqrt(HEAD))
        scores = jnp.where(allowed, scores, -1e30)
        weights = jnp.exp(scores - jnp.max(scores, 0, keepdims=True))
        denoms[h] = jnp.broadcast_to(jnp.sum(weights, 0, keepdims=True), (8, ROWS))
        probs[h] = weights.astype(BF16)

    received(power_x.at[pl.ds(0, NX - 1)], 6)
    received(power_x.at[pl.ds(0, NX)], 7)
    totals = []
    for half in range(2):
        total = power_x[half * NX]
        for k in range(1, NX):
            total = total + power_x[half * NX + k]
        totals.append(total[:NX])
    power_mp[mp] = jnp.concatenate(totals, 0)

    def share_power(k, carry):
        send(power_mp.at[mp], power_mp.at[mp], 12, {"mp": mp_peer(k)}, 13)
        return carry

    lax.fori_loop(0, n_mp - 1, share_power, 0)

    for h in range(NX):
        received(value_all.at[:, h], 8 + h)
        mixer_out[:, pl.ds(h * HEAD, HEAD)] = value_all[SPAN, h].astype(F32).T.astype(BF16)
    mixer_copy = fetch(mixer_out, mixer_hbm, 12)

    received(power_mp.at[pl.ds(0, n_mp - 1)], 12)
    scales[...] = lax.rsqrt(jnp.sum(power_mp[...], 0) * (1.0 / model) + 1e-06)
    for h in range(NX):
        values = [
            (value_all[j, h].astype(F32) * scales[pl.ds(x + j, 1), :]).astype(BF16) for j in range(SPAN + 1)
        ]
        summed = jnp.dot(jnp.concatenate(values, 1), probs[h], preferred_element_type=F32)
        attended_out[:, pl.ds(h * HEAD, HEAD)] = (summed / denoms[h][0:1]).T.astype(BF16)
    attended_copy = fetch(attended_out, attended_hbm, 13)

    sent(recv_taps.at[remote_rows], 0)
    sent(recv_signal.at[remote_rows], 1)
    sent(gate_head.at[pl.ds(0, NX - 1)], 2)
    sent(oldest_keys, 3)
    sent(key_all.at[pl.ds(0, (NX - 1) * ROWS)], 4)
    sent(back_send.at[pl.ds(0, (n_y - 1) * NX)], 5)
    sent(power_x.at[pl.ds(0, NX - 1)], 6)
    sent(power_x.at[pl.ds(0, NX)], 7)
    sent(value_all.at[:, pl.ds(0, 2)], 8)
    for px in range(NX):
        @pl.when(x != px)
        def _():
            sent(value_row.at[pl.ds(0, px + 1)], 9 + px)
    sent(power_mp.at[pl.ds(0, n_mp - 1)], 13)
    mixer_copy.wait()
    attended_copy.wait()


def solution(mesh):
    blocks, n_mp = mesh.shape["ctx"], mesh.shape["mp"]
    constants = tables(blocks)

    def local(gate_in, value_in, gate_out, filter_taps, skip_gain, queries, key_rows):
        rows, lanes = gate_in.shape
        width = lanes // blocks
        n_y = blocks // NX
        hbm = pl.BlockSpec(memory_space=pltpu.HBM)
        square = (NX, ROWS, HEAD)
        return pl.pallas_call(
            functools.partial(kernel, blocks, n_mp, n_mp * lanes),
            out_shape=(jax.ShapeDtypeStruct((rows, lanes), BF16),) * 2,
            in_specs=[hbm] * 12,
            out_specs=(hbm, hbm),
            scratch_shapes=[
                *(pltpu.VMEM((rows, lanes), BF16),) * 3,
                pltpu.VMEM((rows, lanes), F32),
                pltpu.VMEM((rows, lanes), BF16),
                pltpu.SMEM((lanes,), F32),
                *(pltpu.VMEM(c.shape, c.dtype) for c in constants),
                *(pltpu.VMEM((lanes, ROWS), BF16),) * 5,
                pltpu.VMEM((lanes, ROWS), F32),
                pltpu.VMEM((lanes, 2 * ROWS), F32),
                pltpu.VMEM(square, BF16),
                pltpu.VMEM((blocks, width, ROWS), BF16),
                pltpu.VMEM((NX, n_y, width, ROWS), BF16),
                pltpu.VMEM(((SPAN + 1) * ROWS, lanes), BF16),
                pltpu.VMEM(square, BF16),
                pltpu.VMEM((SPAN + 1, NX, HEAD, ROWS), BF16),
                pltpu.VMEM((NX, (SPAN + 1) * ROWS, ROWS), BF16),
                pltpu.VMEM((NX, 8, ROWS), F32),
                pltpu.VMEM((2 * NX, 8, ROWS), F32),
                pltpu.VMEM((n_mp, 8, ROWS), F32),
                pltpu.VMEM((8, ROWS), F32),
                *(pltpu.VMEM((rows, lanes), BF16),) * 2,
                pltpu.SemaphoreType.DMA((14,)),
                pltpu.SemaphoreType.DMA((14,)),
                pltpu.SemaphoreType.DMA((13,)),
            ],
            compiler_params=pltpu.CompilerParams(
                collective_id=0, has_side_effects=True, vmem_limit_bytes=60 * 2**20
            ),
            cost_estimate=pl.CostEstimate(flops=2 * 10**9, bytes_accessed=2 * 10**6, transcendentals=4 * 10**5),
        )(gate_in, value_in, gate_out, filter_taps, queries, key_rows, skip_gain, *constants)

    return jax.shard_map(
        local,
        mesh=mesh,
        in_specs=(P("ctx", "mp"),) * 4 + (P("mp"),) + (P("ctx", "mp"),) * 2,
        out_specs=(P("ctx", "mp"), P("ctx", "mp")),
        check_vma=False,
    )
```

```python
import functools
import math

import jax
import jax.numpy as jnp
import ml_dtypes
import numpy as np
from jax import lax
from jax.experimental import pallas as pl
from jax.experimental.pallas import tpu as pltpu
from jax.sharding import PartitionSpec as P

HEAD = 128
ROWS = 128
SPAN = 4
NX = 4
MESH = pl.DeviceIdType.MESH
F32 = jnp.float32
BF16 = jnp.bfloat16


def split(table):
    high = table.astype(np.float32).astype(ml_dtypes.bfloat16)
    low = (table - high.astype(np.float64)).astype(np.float32).astype(ml_dtypes.bfloat16)
    return high, low


def tables(blocks):
    length = blocks * ROWS
    n1 = np.arange(blocks)[None, :]
    k1 = np.arange(blocks)[:, None] + 0.25
    n2 = np.arange(ROWS)[None, :]
    first = np.exp(-2j * np.pi * n1 * k1 / blocks)
    twist = np.exp(-2j * np.pi * n2 * k1 / length)
    second = np.exp(-2j * np.pi * n2 * n2.T / ROWS)
    first_high, first_low = split(np.concatenate([first.real, first.imag], 0))
    first_cat = np.concatenate([first_high, first_low], 1)
    wide = np.block([[second.real, second.imag], [-second.imag, second.real]])
    wide_high, wide_low = split(wide)
    last_high, last_low = split(np.concatenate([first.real, first.imag], 0).T / length)
    last_cat = np.concatenate([last_high, last_low, last_high], 1)
    twists = np.stack([twist.real, twist.imag]).astype(np.float32)
    return first_cat, twists, wide_high, wide_low, last_cat


def halves(value):
    high = value.astype(BF16)
    return high, (value - high.astype(F32)).astype(BF16)


def kernel(
    blocks, n_mp, model,
    gate_hbm, value_hbm, out_gate_hbm, taps_hbm, query_hbm, key_hbm, skip_hbm,
    first_hbm, twist_hbm, wide_high_hbm, wide_low_hbm, last_hbm,
    mixer_hbm, attended_hbm,
    gate_ref, value_ref, out_gate_ref, taps_ref, query_ref, skip_ref,
    first_ref, twist_ref, wide_high_ref, wide_low_ref, last_ref,
    send_taps, send_signal, send_gate, recv_taps, recv_signal, work, spectrum,
    gate_head, back_send, back_recv, key_all, value_row, value_old, value_all, probs, denoms,
    power_x, power_mp, scales, mixer_out, attended_out,
    local_sems, send_sems, recv_sems,
):
    me = lax.axis_index("ctx")
    mp = lax.axis_index("mp")
    x, y = lax.rem(me, NX), lax.div(me, NX)
    n_y = blocks // NX
    width = NX * HEAD // blocks

    def far_first(k, count):
        half = lax.div(k + 1, 2)
        return lax.rem(count // 2 + jnp.where(lax.rem(k, 2) == 1, half, count - half), count)

    def ctx_peer(k):
        px = lax.rem(x + far_first(lax.rem(k, NX), NX), NX)
        py = lax.rem(y + far_first(lax.div(k, NX), n_y), n_y)
        return py * NX + px

    def mp_peer(k):
        return lax.rem(mp + far_first(k, n_mp), n_mp)

    barrier = pltpu.get_barrier_semaphore()

    def greet_ctx(k, carry):
        pl.semaphore_signal(barrier, inc=1, device_id={"ctx": ctx_peer(k)}, device_id_type=MESH)
        return carry

    def greet_mp(k, carry):
        pl.semaphore_signal(barrier, inc=1, device_id={"mp": mp_peer(k)}, device_id_type=MESH)
        return carry

    def fetch(src, dst, which):
        copy = pltpu.make_async_copy(src, dst, local_sems.at[which])
        copy.start()
        return copy

    first_loads = [
        fetch(src, dst, which)
        for which, (src, dst) in enumerate([(taps_hbm, taps_ref), (gate_hbm, gate_ref), (value_hbm, value_ref)])
    ]
    lax.fori_loop(0, blocks - 1, greet_ctx, 0)
    lax.fori_loop(0, n_mp - 1, greet_mp, 0)
    own_rows = pl.ds(SPAN * ROWS, ROWS)
    loads = [
        fetch(src, dst, 3 + which)
        for which, (src, dst) in enumerate([
            (out_gate_hbm, out_gate_ref), (first_hbm, first_ref), (twist_hbm, twist_ref),
            (wide_high_hbm, wide_high_ref), (wide_low_hbm, wide_low_ref), (last_hbm, last_ref), (skip_hbm, skip_ref),
            (query_hbm, query_ref), (key_hbm, key_all.at[own_rows]),
        ])
    ]

    def send(src, dst, which, target, send_which=None):
        pltpu.make_async_remote_copy(
            src_ref=src, dst_ref=dst, send_sem=send_sems.at[which if send_which is None else send_which],
            recv_sem=recv_sems.at[which], device_id=target, device_id_type=MESH,
        ).start()

    def received(ref, which):
        pltpu.make_async_copy(ref, ref, recv_sems.at[which]).wait()

    def sent(ref, which):
        pltpu.make_async_copy(ref, ref, send_sems.at[which]).wait()

    def group(d):
        return pl.ds(pl.multiple_of(lax.rem(d, NX) * HEAD + lax.div(d, NX) * width, width), width)

    mine = pl.ds(pl.multiple_of(me * width, width), width)
    my_lanes = pl.ds(pl.multiple_of(x * HEAD, HEAD), HEAD)

    first_loads[0].wait()
    send_taps[...] = taps_ref[...].T.astype(BF16)
    first_loads[1].wait()
    first_loads[2].wait()
    send_signal[...] = (gate_ref[...].astype(F32) * value_ref[...].astype(F32)).T.astype(BF16)
    pl.semaphore_wait(barrier, blocks - 1 + n_mp - 1)

    def spread(which, src, dst):
        def step(k, carry):
            d = ctx_peer(k)
            send(src.at[group(d)], dst.at[mine], which, {"ctx": d})
            return carry
        lax.fori_loop(0, blocks - 1, step, 0)
        dst[mine] = src[group(me)]

    spread(0, send_taps, recv_taps)
    spread(1, send_signal, recv_signal)

    loads[-1].wait()
    next_row = lax.rem(me + NX, blocks)
    own_keys, oldest_keys = key_all.at[own_rows], key_all.at[pl.ds(0, ROWS)]
    send(own_keys, oldest_keys, 3, {"ctx": next_row})
    for px in range(1, NX):
        @pl.when(x < px)
        def _():
            slot = pl.multiple_of((SPAN + x - px) * ROWS, ROWS)
            send(own_keys, key_all.at[pl.ds(slot, ROWS)], 4, {"ctx": y * NX + px})

    loads[0].wait()
    send_gate[...] = out_gate_ref[...].astype(F32).T.astype(BF16)
    for k in (2, 1, 3):
        px = lax.rem(x + k, NX)
        lanes = pl.ds(pl.multiple_of(px * HEAD, HEAD), HEAD)
        send(send_gate.at[lanes], gate_head.at[x], 2, {"ctx": y * NX + px})
    gate_head[x] = send_gate[my_lanes]

    for load in loads[1:-1]:
        load.wait()
    twist_real, twist_imag = twist_ref[0], twist_ref[1]

    def times_wide(value, contract):
        high, low = halves(value)
        dims = (((1,), (contract,)), ((), ()))

        def dot(a, b):
            return lax.dot_general(a, b, dims, preferred_element_type=F32)

        return dot(high, wide_high_ref[...]) + dot(low, wide_high_ref[...]) + dot(high, wide_low_ref[...])

    def lane_tile(value, c):
        return value[:, c * ROWS:(c + 1) * ROWS]

    def forward(recv):
        work[...] = recv[...].astype(F32)
        panel = jnp.concatenate([work[pl.ds(c, blocks, stride=width), :] for c in range(width)], 1).astype(BF16)
        panel = jnp.concatenate([panel, panel], 0)
        bins = jnp.dot(first_ref[...], panel, preferred_element_type=F32)
        real, imag = bins[:blocks], bins[blocks:]
        rows = []
        for c in range(width):
            a, b = lane_tile(real, c), lane_tile(imag, c)
            rows.append(jnp.concatenate([a * twist_real - b * twist_imag, a * twist_imag + b * twist_real], 1))
        return times_wide(jnp.concatenate(rows, 0), 0)

    remote_rows = pl.ds(0, (blocks - 1) * width)
    received(recv_taps.at[remote_rows], 0)
    spectrum[...] = forward(recv_taps)
    skip_at = x * HEAD + y * width
    for c in range(width):
        rows = pl.ds(c * blocks, blocks)
        spectrum[rows, pl.ds(0, ROWS)] = spectrum[rows, pl.ds(0, ROWS)] + skip_ref[skip_at + c]
    received(recv_signal.at[remote_rows], 1)

    bins = forward(recv_signal)
    a, b = bins[:, :ROWS], bins[:, ROWS:]
    c, d = spectrum[:, pl.ds(0, ROWS)], spectrum[:, pl.ds(ROWS, ROWS)]
    back = times_wide(jnp.concatenate([a * c - b * d, a * d + b * c], 1), 1)
    columns = []
    for c in range(width):
        part = back[c * blocks:(c + 1) * blocks]
        a, b = part[:, :ROWS], part[:, ROWS:]
        columns.append(jnp.concatenate([a * twist_real + b * twist_imag, b * twist_real - a * twist_imag], 0))
    high, low = halves(jnp.concatenate(columns, 1))
    convolved = jnp.dot(last_ref[...], jnp.concatenate([high, high, low], 0), preferred_element_type=F32)
    for c in range(width):
        work[pl.ds(c, blocks, stride=width), :] = lane_tile(convolved, c)
    back_send[...] = work[...].astype(BF16).reshape(blocks, width, ROWS)

    def send_back(k, carry):
        py = lax.rem(y + far_first(k, n_y), n_y)
        send(back_send.at[pl.ds(py * NX, NX)], back_recv.at[:, y], 5, {"ctx": py * NX + x})
        return carry

    lax.fori_loop(0, n_y - 1, send_back, 0)
    back_recv[:, y] = back_send[pl.ds(y * NX, NX)]

    received(oldest_keys, 3)
    for px in range(NX - 1):
        @pl.when(x > px)
        def _():
            slot = pl.multiple_of((x - px) * ROWS, ROWS)
            send(oldest_keys, key_all.at[pl.ds(slot, ROWS)], 4, {"ctx": y * NX + px})

    received(gate_head.at[pl.ds(0, NX - 1)], 2)
    received(back_send.at[pl.ds(0, (n_y - 1) * NX)], 5)
    gated = gate_head[...].astype(F32) * back_recv[...].reshape(NX, HEAD, ROWS).astype(F32)
    mixed = gated.astype(BF16)
    value_row[...] = mixed
    widened = mixed.astype(F32)
    power = jnp.sum(widened * widened, 1)
    power_x[NX + x] = jnp.concatenate([power, jnp.zeros_like(power)], 0)
    next_y = lax.rem(y + 1, n_y)
    for k in (2, 1, 3, 0):
        px = lax.rem(x + k, NX)
        send(power_x.at[NX + x], power_x.at[x], 7, {"ctx": next_y * NX + px})
        if k:
            send(power_x.at[NX + x], power_x.at[NX + x], 6, {"ctx": y * NX + px})
    send(value_row, value_old, 13, {"ctx": next_row}, 8)
    for px in range(NX):
        src, dst = value_row.at[pl.ds(0, px + 1)], value_all.at[pl.ds(SPAN - px, px + 1), x]

        @pl.when(x != px)
        def _():
            send(src, dst, 8 + x, {"ctx": y * NX + px}, 9 + px)

        @pl.when(x == px)
        def _():
            pltpu.make_async_copy(src, dst, recv_sems.at[8 + x]).start()

    received(power_x.at[pl.ds(0, NX - 1)], 6)
    received(power_x.at[pl.ds(0, NX)], 7)
    totals = []
    for half in range(2):
        total = power_x[half * NX]
        for k in range(1, NX):
            total = total + power_x[half * NX + k]
        totals.append(total[:NX])
    power_mp[mp] = jnp.concatenate(totals, 0)

    def share_power(k, carry):
        send(power_mp.at[mp], power_mp.at[mp], 12, {"mp": mp_peer(k)}, 13)
        return carry

    lax.fori_loop(0, n_mp - 1, share_power, 0)

    received(value_old, 13)
    for px in range(NX):
        src, dst = value_old.at[pl.ds(px, NX - px)], value_all.at[pl.ds(0, NX - px), x]

        @pl.when(x != px)
        def _():
            send(src, dst, 8 + x, {"ctx": y * NX + px}, 14 + px)

        @pl.when(x == px)
        def _():
            pltpu.make_async_copy(src, dst, recv_sems.at[8 + x]).start()

    received(key_all.at[pl.ds(0, (NX - 1) * ROWS)], 4)
    reach = (SPAN + 1) * ROWS
    key_at = lax.broadcasted_iota(jnp.int32, (reach, ROWS), 0)
    query_at = lax.broadcasted_iota(jnp.int32, (reach, ROWS), 1)
    first_key = jnp.maximum(SPAN - me, 0) * ROWS
    allowed = (key_at > query_at) & (key_at <= query_at + SPAN * ROWS) & (key_at >= first_key)
    for h in range(NX):
        lanes = pl.ds(h * HEAD, HEAD)
        scores = lax.dot_general(
            key_all[:, lanes], query_ref[:, lanes], (((1,), (1,)), ((), ())), preferred_element_type=F32
        ) * (1.0 / math.sqrt(HEAD))
        scores = jnp.where(allowed, scores, -1e30)
        weights = jnp.exp(scores - jnp.max(scores, 0, keepdims=True))
        denoms[h] = jnp.broadcast_to(jnp.sum(weights, 0, keepdims=True), (8, ROWS))
        probs[h] = weights.astype(BF16)

    for h in range(NX):
        received(value_all.at[:, h], 8 + h)
        mixer_out[:, pl.ds(h * HEAD, HEAD)] = value_all[SPAN, h].astype(F32).T.astype(BF16)
    mixer_copy = fetch(mixer_out, mixer_hbm, 12)

    received(power_mp.at[pl.ds(0, n_mp - 1)], 12)
    scales[...] = lax.rsqrt(jnp.sum(power_mp[...], 0) * (1.0 / model) + 1e-06)
    for h in range(NX):
        values = [
            (value_all[j, h].astype(F32) * scales[pl.ds(x + j, 1), :]).astype(BF16) for j in range(SPAN + 1)
        ]
        summed = jnp.dot(jnp.concatenate(values, 1), probs[h], preferred_element_type=F32)
        attended_out[:, pl.ds(h * HEAD, HEAD)] = (summed / denoms[h][0:1]).T.astype(BF16)
    attended_copy = fetch(attended_out, attended_hbm, 13)

    sent(recv_taps.at[remote_rows], 0)
    sent(recv_signal.at[remote_rows], 1)
    sent(gate_head.at[pl.ds(0, NX - 1)], 2)
    sent(oldest_keys, 3)
    sent(key_all.at[pl.ds(0, (NX - 1) * ROWS)], 4)
    sent(back_send.at[pl.ds(0, (n_y - 1) * NX)], 5)
    sent(power_x.at[pl.ds(0, NX - 1)], 6)
    sent(power_x.at[pl.ds(0, NX)], 7)
    sent(value_row, 8)
    for px in range(NX):
        @pl.when(x != px)
        def _():
            sent(value_row.at[pl.ds(0, px + 1)], 9 + px)
            sent(value_row.at[pl.ds(0, NX - px)], 14 + px)
    sent(power_mp.at[pl.ds(0, n_mp - 1)], 13)
    mixer_copy.wait()
    attended_copy.wait()


def solution(mesh):
    blocks, n_mp = mesh.shape["ctx"], mesh.shape["mp"]
    constants = tables(blocks)

    def local(gate_in, value_in, gate_out, filter_taps, skip_gain, queries, key_rows):
        rows, lanes = gate_in.shape
        width = lanes // blocks
        n_y = blocks // NX
        hbm = pl.BlockSpec(memory_space=pltpu.HBM)
        square = (NX, ROWS, HEAD)
        return pl.pallas_call(
            functools.partial(kernel, blocks, n_mp, n_mp * lanes),
            out_shape=(jax.ShapeDtypeStruct((rows, lanes), BF16),) * 2,
            in_specs=[hbm] * 12,
            out_specs=(hbm, hbm),
            scratch_shapes=[
                *(pltpu.VMEM((rows, lanes), BF16),) * 3,
                pltpu.VMEM((rows, lanes), F32),
                pltpu.VMEM((rows, lanes), BF16),
                pltpu.SMEM((lanes,), F32),
                *(pltpu.VMEM(c.shape, c.dtype) for c in constants),
                *(pltpu.VMEM((lanes, ROWS), BF16),) * 5,
                pltpu.VMEM((lanes, ROWS), F32),
                pltpu.VMEM((lanes, 2 * ROWS), F32),
                pltpu.VMEM(square, BF16),
                pltpu.VMEM((blocks, width, ROWS), BF16),
                pltpu.VMEM((NX, n_y, width, ROWS), BF16),
                pltpu.VMEM(((SPAN + 1) * ROWS, lanes), BF16),
                pltpu.VMEM(square, BF16),
                pltpu.VMEM(square, BF16),
                pltpu.VMEM((SPAN + 1, NX, HEAD, ROWS), BF16),
                pltpu.VMEM((NX, (SPAN + 1) * ROWS, ROWS), BF16),
                pltpu.VMEM((NX, 8, ROWS), F32),
                pltpu.VMEM((2 * NX, 8, ROWS), F32),
                pltpu.VMEM((n_mp, 8, ROWS), F32),
                pltpu.VMEM((8, ROWS), F32),
                *(pltpu.VMEM((rows, lanes), BF16),) * 2,
                pltpu.SemaphoreType.DMA((14,)),
                pltpu.SemaphoreType.DMA((18,)),
                pltpu.SemaphoreType.DMA((14,)),
            ],
            compiler_params=pltpu.CompilerParams(
                collective_id=0, has_side_effects=True, vmem_limit_bytes=60 * 2**20
            ),
            cost_estimate=pl.CostEstimate(flops=2 * 10**9, bytes_accessed=2 * 10**6, transcendentals=4 * 10**5),
        )(gate_in, value_in, gate_out, filter_taps, queries, key_rows, skip_gain, *constants)

    return jax.shard_map(
        local,
        mesh=mesh,
        in_specs=(P("ctx", "mp"),) * 4 + (P("mp"),) + (P("ctx", "mp"),) * 2,
        out_specs=(P("ctx", "mp"), P("ctx", "mp")),
        check_vma=False,
    )
```

```python
import functools
import math

import jax
import jax.numpy as jnp
import ml_dtypes
import numpy as np
from jax import lax
from jax.experimental import pallas as pl
from jax.experimental.pallas import tpu as pltpu
from jax.sharding import PartitionSpec as P

HEAD = 128
ROWS = 128
SPAN = 4
NX = 4
MESH = pl.DeviceIdType.MESH
F32 = jnp.float32
BF16 = jnp.bfloat16


def split(table):
    high = table.astype(np.float32).astype(ml_dtypes.bfloat16)
    low = (table - high.astype(np.float64)).astype(np.float32).astype(ml_dtypes.bfloat16)
    return high, low


def tables(blocks):
    length = blocks * ROWS
    n1 = np.arange(blocks)[None, :]
    k1 = np.arange(blocks)[:, None] + 0.25
    n2 = np.arange(ROWS)[None, :]
    first = np.exp(-2j * np.pi * n1 * k1 / blocks)
    twist = np.exp(-2j * np.pi * n2 * k1 / length)
    second = np.exp(-2j * np.pi * n2 * n2.T / ROWS)
    first_high, first_low = split(np.concatenate([first.real, first.imag], 0))
    first_cat = np.concatenate([first_high, first_low], 1)
    wide = np.block([[second.real, second.imag], [-second.imag, second.real]])
    wide_high, wide_low = split(wide)
    last_high, last_low = split(np.concatenate([first.real, first.imag], 0).T / length)
    last_cat = np.concatenate([last_high, last_low, last_high], 1)
    twists = np.stack([twist.real, twist.imag]).astype(np.float32)
    return first_cat, twists, wide_high, wide_low, last_cat


def halves(value):
    high = value.astype(BF16)
    return high, (value - high.astype(F32)).astype(BF16)


def kernel(
    blocks, n_mp, model,
    gate_hbm, value_hbm, out_gate_hbm, taps_hbm, query_hbm, key_hbm, skip_hbm,
    first_hbm, twist_hbm, wide_high_hbm, wide_low_hbm, last_hbm,
    mixer_out, attended_out,
    gate_ref, value_ref, out_gate_ref, taps_ref, query_ref, skip_ref,
    first_ref, twist_ref, wide_high_ref, wide_low_ref, last_ref,
    send_taps, send_signal, send_gate, recv_taps, recv_signal, work, spectrum,
    gate_head, back_send, back_recv, key_all, value_row, value_old, value_all, probs, denoms,
    power_x, power_mp, scales,
    local_sems, send_sems, recv_sems,
):
    me = lax.axis_index("ctx")
    mp = lax.axis_index("mp")
    x, y = lax.rem(me, NX), lax.div(me, NX)
    n_y = blocks // NX
    width = NX * HEAD // blocks

    def far_first(k, count):
        half = lax.div(k + 1, 2)
        return lax.rem(count // 2 + jnp.where(lax.rem(k, 2) == 1, half, count - half), count)

    def ctx_peer(k):
        px = lax.rem(x + far_first(lax.rem(k, NX), NX), NX)
        py = lax.rem(y + far_first(lax.div(k, NX), n_y), n_y)
        return py * NX + px

    def mp_peer(k):
        return lax.rem(mp + far_first(k, n_mp), n_mp)

    barrier = pltpu.get_barrier_semaphore()

    def greet_ctx(k, carry):
        pl.semaphore_signal(barrier, inc=1, device_id={"ctx": ctx_peer(k)}, device_id_type=MESH)
        return carry

    def greet_mp(k, carry):
        pl.semaphore_signal(barrier, inc=1, device_id={"mp": mp_peer(k)}, device_id_type=MESH)
        return carry

    def fetch(src, dst, which):
        copy = pltpu.make_async_copy(src, dst, local_sems.at[which])
        copy.start()
        return copy

    first_loads = [
        fetch(src, dst, which)
        for which, (src, dst) in enumerate([(taps_hbm, taps_ref), (gate_hbm, gate_ref), (value_hbm, value_ref)])
    ]
    lax.fori_loop(0, blocks - 1, greet_ctx, 0)
    lax.fori_loop(0, n_mp - 1, greet_mp, 0)
    own_rows = pl.ds(SPAN * ROWS, ROWS)
    loads = [
        fetch(src, dst, 3 + which)
        for which, (src, dst) in enumerate([
            (out_gate_hbm, out_gate_ref), (first_hbm, first_ref), (twist_hbm, twist_ref),
            (wide_high_hbm, wide_high_ref), (wide_low_hbm, wide_low_ref), (last_hbm, last_ref), (skip_hbm, skip_ref),
            (query_hbm, query_ref), (key_hbm, key_all.at[own_rows]),
        ])
    ]

    def send(src, dst, which, target, send_which=None):
        pltpu.make_async_remote_copy(
            src_ref=src, dst_ref=dst, send_sem=send_sems.at[which if send_which is None else send_which],
            recv_sem=recv_sems.at[which], device_id=target, device_id_type=MESH,
        ).start()

    def received(ref, which):
        pltpu.make_async_copy(ref, ref, recv_sems.at[which]).wait()

    def sent(ref, which):
        pltpu.make_async_copy(ref, ref, send_sems.at[which]).wait()

    def group(d):
        return pl.ds(pl.multiple_of(lax.rem(d, NX) * HEAD + lax.div(d, NX) * width, width), width)

    mine = pl.ds(pl.multiple_of(me * width, width), width)
    my_lanes = pl.ds(pl.multiple_of(x * HEAD, HEAD), HEAD)

    first_loads[0].wait()
    send_taps[...] = taps_ref[...].T.astype(BF16)
    first_loads[1].wait()
    first_loads[2].wait()
    send_signal[...] = (gate_ref[...].astype(F32) * value_ref[...].astype(F32)).T.astype(BF16)
    pl.semaphore_wait(barrier, blocks - 1 + n_mp - 1)

    def spread(which, src, dst):
        def step(k, carry):
            d = ctx_peer(k)
            send(src.at[group(d)], dst.at[mine], which, {"ctx": d})
            return carry
        lax.fori_loop(0, blocks - 1, step, 0)
        dst[mine] = src[group(me)]

    spread(0, send_taps, recv_taps)
    spread(1, send_signal, recv_signal)

    loads[-1].wait()
    next_row = lax.rem(me + NX, blocks)
    own_keys, oldest_keys = key_all.at[own_rows], key_all.at[pl.ds(0, ROWS)]
    send(own_keys, oldest_keys, 3, {"ctx": next_row})
    for px in range(1, NX):
        @pl.when(x < px)
        def _():
            slot = pl.multiple_of((SPAN + x - px) * ROWS, ROWS)
            send(own_keys, key_all.at[pl.ds(slot, ROWS)], 4, {"ctx": y * NX + px})

    loads[0].wait()
    send_gate[...] = out_gate_ref[...].astype(F32).T.astype(BF16)
    for k in (2, 1, 3):
        px = lax.rem(x + k, NX)
        lanes = pl.ds(pl.multiple_of(px * HEAD, HEAD), HEAD)
        send(send_gate.at[lanes], gate_head.at[x], 2, {"ctx": y * NX + px})
    gate_head[x] = send_gate[my_lanes]

    for load in loads[1:-1]:
        load.wait()
    twist_real, twist_imag = twist_ref[0], twist_ref[1]

    def times_wide(value, contract):
        high, low = halves(value)
        dims = (((1,), (contract,)), ((), ()))

        def dot(a, b):
            return lax.dot_general(a, b, dims, preferred_element_type=F32)

        return dot(high, wide_high_ref[...]) + dot(low, wide_high_ref[...]) + dot(high, wide_low_ref[...])

    def lane_tile(value, c):
        return value[:, c * ROWS:(c + 1) * ROWS]

    def forward(recv):
        work[...] = recv[...].astype(F32)
        panel = jnp.concatenate([work[pl.ds(c, blocks, stride=width), :] for c in range(width)], 1).astype(BF16)
        panel = jnp.concatenate([panel, panel], 0)
        bins = jnp.dot(first_ref[...], panel, preferred_element_type=F32)
        real, imag = bins[:blocks], bins[blocks:]
        rows = []
        for c in range(width):
            a, b = lane_tile(real, c), lane_tile(imag, c)
            rows.append(jnp.concatenate([a * twist_real - b * twist_imag, a * twist_imag + b * twist_real], 1))
        return times_wide(jnp.concatenate(rows, 0), 0)

    remote_rows = pl.ds(0, (blocks - 1) * width)
    received(recv_taps.at[remote_rows], 0)
    spectrum[...] = forward(recv_taps)
    skip_at = x * HEAD + y * width
    for c in range(width):
        rows = pl.ds(c * blocks, blocks)
        spectrum[rows, pl.ds(0, ROWS)] = spectrum[rows, pl.ds(0, ROWS)] + skip_ref[skip_at + c]
    received(recv_signal.at[remote_rows], 1)

    bins = forward(recv_signal)
    a, b = bins[:, :ROWS], bins[:, ROWS:]
    c, d = spectrum[:, pl.ds(0, ROWS)], spectrum[:, pl.ds(ROWS, ROWS)]
    back = times_wide(jnp.concatenate([a * c - b * d, a * d + b * c], 1), 1)
    columns = []
    for c in range(width):
        part = back[c * blocks:(c + 1) * blocks]
        a, b = part[:, :ROWS], part[:, ROWS:]
        columns.append(jnp.concatenate([a * twist_real + b * twist_imag, b * twist_real - a * twist_imag], 0))
    high, low = halves(jnp.concatenate(columns, 1))
    convolved = jnp.dot(last_ref[...], jnp.concatenate([high, high, low], 0), preferred_element_type=F32)
    for c in range(width):
        work[pl.ds(c, blocks, stride=width), :] = lane_tile(convolved, c)
    back_send[...] = work[...].astype(BF16).reshape(blocks, width, ROWS)

    def send_back(k, carry):
        py = lax.rem(y + far_first(k, n_y), n_y)
        send(back_send.at[pl.ds(py * NX, NX)], back_recv.at[:, y], 5, {"ctx": py * NX + x})
        return carry

    lax.fori_loop(0, n_y - 1, send_back, 0)
    back_recv[:, y] = back_send[pl.ds(y * NX, NX)]

    received(oldest_keys, 3)
    for px in range(NX - 1):
        @pl.when(x > px)
        def _():
            slot = pl.multiple_of((x - px) * ROWS, ROWS)
            send(oldest_keys, key_all.at[pl.ds(slot, ROWS)], 4, {"ctx": y * NX + px})

    received(gate_head.at[pl.ds(0, NX - 1)], 2)
    received(back_send.at[pl.ds(0, (n_y - 1) * NX)], 5)
    gated = gate_head[...].astype(F32) * back_recv[...].reshape(NX, HEAD, ROWS).astype(F32)
    mixed = gated.astype(BF16)
    value_row[...] = mixed
    widened = mixed.astype(F32)
    power = jnp.sum(widened * widened, 1)
    power_x[NX + x] = jnp.concatenate([power, jnp.zeros_like(power)], 0)
    next_y = lax.rem(y + 1, n_y)
    for k in (2, 1, 3, 0):
        px = lax.rem(x + k, NX)
        send(power_x.at[NX + x], power_x.at[x], 7, {"ctx": next_y * NX + px})
        if k:
            send(power_x.at[NX + x], power_x.at[NX + x], 6, {"ctx": y * NX + px})
    send(value_row, value_old, 13, {"ctx": next_row}, 8)
    for px in range(NX):
        src, dst = value_row.at[pl.ds(0, px + 1)], value_all.at[pl.ds(SPAN - px, px + 1), x]

        @pl.when(x != px)
        def _():
            send(src, dst, 8 + x, {"ctx": y * NX + px}, 9 + px)

        @pl.when(x == px)
        def _():
            pltpu.make_async_copy(src, dst, recv_sems.at[8 + x]).start()

    received(power_x.at[pl.ds(0, NX - 1)], 6)
    received(power_x.at[pl.ds(0, NX)], 7)
    totals = []
    for half in range(2):
        total = power_x[half * NX]
        for k in range(1, NX):
            total = total + power_x[half * NX + k]
        totals.append(total[:NX])
    power_mp[mp] = jnp.concatenate(totals, 0)

    def share_power(k, carry):
        send(power_mp.at[mp], power_mp.at[mp], 12, {"mp": mp_peer(k)}, 13)
        return carry

    lax.fori_loop(0, n_mp - 1, share_power, 0)

    received(value_old, 13)
    for px in range(NX):
        src, dst = value_old.at[pl.ds(px, NX - px)], value_all.at[pl.ds(0, NX - px), x]

        @pl.when(x != px)
        def _():
            send(src, dst, 8 + x, {"ctx": y * NX + px}, 14 + px)

        @pl.when(x == px)
        def _():
            pltpu.make_async_copy(src, dst, recv_sems.at[8 + x]).start()

    received(key_all.at[pl.ds(0, (NX - 1) * ROWS)], 4)
    reach = (SPAN + 1) * ROWS
    key_at = lax.broadcasted_iota(jnp.int32, (reach, ROWS), 0)
    query_at = lax.broadcasted_iota(jnp.int32, (reach, ROWS), 1)
    first_key = jnp.maximum(SPAN - me, 0) * ROWS
    allowed = (key_at > query_at) & (key_at <= query_at + SPAN * ROWS) & (key_at >= first_key)
    for h in range(NX):
        lanes = pl.ds(h * HEAD, HEAD)
        scores = lax.dot_general(
            key_all[:, lanes], query_ref[:, lanes], (((1,), (1,)), ((), ())), preferred_element_type=F32
        ) * (1.0 / math.sqrt(HEAD))
        scores = jnp.where(allowed, scores, -1e30)
        weights = jnp.exp(scores - jnp.max(scores, 0, keepdims=True))
        denoms[h] = jnp.broadcast_to(jnp.sum(weights, 0, keepdims=True), (8, ROWS))
        probs[h] = weights.astype(BF16)

    for h in range(NX):
        received(value_all.at[:, h], 8 + h)
        mixer_out[:, pl.ds(h * HEAD, HEAD)] = value_all[SPAN, h].astype(F32).T.astype(BF16)

    received(power_mp.at[pl.ds(0, n_mp - 1)], 12)
    scales[...] = lax.rsqrt(jnp.sum(power_mp[...], 0) * (1.0 / model) + 1e-06)
    for h in range(NX):
        values = [
            (value_all[j, h].astype(F32) * scales[pl.ds(x + j, 1), :]).astype(BF16) for j in range(SPAN + 1)
        ]
        summed = jnp.dot(jnp.concatenate(values, 1), probs[h], preferred_element_type=F32)
        attended_out[:, pl.ds(h * HEAD, HEAD)] = (summed / denoms[h][0:1]).T.astype(BF16)

    sent(recv_taps.at[remote_rows], 0)
    sent(recv_signal.at[remote_rows], 1)
    sent(gate_head.at[pl.ds(0, NX - 1)], 2)
    sent(oldest_keys, 3)
    sent(key_all.at[pl.ds(0, (NX - 1) * ROWS)], 4)
    sent(back_send.at[pl.ds(0, (n_y - 1) * NX)], 5)
    sent(power_x.at[pl.ds(0, NX - 1)], 6)
    sent(power_x.at[pl.ds(0, NX)], 7)
    sent(value_row, 8)
    for px in range(NX):
        @pl.when(x != px)
        def _():
            sent(value_row.at[pl.ds(0, px + 1)], 9 + px)
            sent(value_row.at[pl.ds(0, NX - px)], 14 + px)
    sent(power_mp.at[pl.ds(0, n_mp - 1)], 13)


def hand_over(mixer_from, attended_from, mixer_to, attended_to, sems):
    copies = [
        pltpu.make_async_copy(mixer_from, mixer_to, sems.at[0]),
        pltpu.make_async_copy(attended_from, attended_to, sems.at[1]),
    ]
    for copy in copies:
        copy.start()
    for copy in copies:
        copy.wait()


def solution(mesh):
    blocks, n_mp = mesh.shape["ctx"], mesh.shape["mp"]
    constants = tables(blocks)

    def local(gate_in, value_in, gate_out, filter_taps, skip_gain, queries, key_rows):
        rows, lanes = gate_in.shape
        width = lanes // blocks
        n_y = blocks // NX
        hbm = pl.BlockSpec(memory_space=pltpu.HBM)
        square = (NX, ROWS, HEAD)
        operands = gate_in, value_in, gate_out, filter_taps, queries, key_rows, skip_gain, *constants
        operands = [pltpu.with_memory_space_constraint(o, pltpu.HBM) for o in operands]
        mixer, attended = pl.pallas_call(
            functools.partial(kernel, blocks, n_mp, n_mp * lanes),
            out_shape=(pltpu.VMEM((rows, lanes), BF16),) * 2,
            in_specs=[hbm] * 12,
            out_specs=(pl.BlockSpec(memory_space=pltpu.VMEM),) * 2,
            scratch_shapes=[
                *(pltpu.VMEM((rows, lanes), BF16),) * 3,
                pltpu.VMEM((rows, lanes), F32),
                pltpu.VMEM((rows, lanes), BF16),
                pltpu.SMEM((lanes,), F32),
                *(pltpu.VMEM(c.shape, c.dtype) for c in constants),
                *(pltpu.VMEM((lanes, ROWS), BF16),) * 5,
                pltpu.VMEM((lanes, ROWS), F32),
                pltpu.VMEM((lanes, 2 * ROWS), F32),
                pltpu.VMEM(square, BF16),
                pltpu.VMEM((blocks, width, ROWS), BF16),
                pltpu.VMEM((NX, n_y, width, ROWS), BF16),
                pltpu.VMEM(((SPAN + 1) * ROWS, lanes), BF16),
                pltpu.VMEM(square, BF16),
                pltpu.VMEM(square, BF16),
                pltpu.VMEM((SPAN + 1, NX, HEAD, ROWS), BF16),
                pltpu.VMEM((NX, (SPAN + 1) * ROWS, ROWS), BF16),
                pltpu.VMEM((NX, 8, ROWS), F32),
                pltpu.VMEM((2 * NX, 8, ROWS), F32),
                pltpu.VMEM((n_mp, 8, ROWS), F32),
                pltpu.VMEM((8, ROWS), F32),
                pltpu.SemaphoreType.DMA((14,)),
                pltpu.SemaphoreType.DMA((18,)),
                pltpu.SemaphoreType.DMA((14,)),
            ],
            compiler_params=pltpu.CompilerParams(
                collective_id=0, has_side_effects=True, vmem_limit_bytes=32 * 2**20
            ),
            cost_estimate=pl.CostEstimate(flops=2 * 10**9, bytes_accessed=2 * 10**6, transcendentals=4 * 10**5),
        )(*operands)
        return pl.pallas_call(
            hand_over,
            out_shape=(jax.ShapeDtypeStruct((rows, lanes), BF16),) * 2,
            in_specs=[pl.BlockSpec(memory_space=pltpu.VMEM)] * 2,
            out_specs=(hbm,) * 2,
            scratch_shapes=[pltpu.SemaphoreType.DMA((2,))],
            compiler_params=pltpu.CompilerParams(vmem_limit_bytes=8 * 2**20),
        )(mixer, attended)

    return jax.shard_map(
        local,
        mesh=mesh,
        in_specs=(P("ctx", "mp"),) * 4 + (P("mp"),) + (P("ctx", "mp"),) * 2,
        out_specs=(P("ctx", "mp"), P("ctx", "mp")),
        check_vma=False,
    )
```

```python
import functools
import math

import jax
import jax.numpy as jnp
import ml_dtypes
import numpy as np
from jax import lax
from jax.experimental import pallas as pl
from jax.experimental.pallas import tpu as pltpu
from jax.sharding import PartitionSpec as P

HEAD = 128
ROWS = 128
SPAN = 4
NX = 4
MESH = pl.DeviceIdType.MESH
F32 = jnp.float32
BF16 = jnp.bfloat16


def split(table):
    high = table.astype(np.float32).astype(ml_dtypes.bfloat16)
    low = (table - high.astype(np.float64)).astype(np.float32).astype(ml_dtypes.bfloat16)
    return high, low


def tables(blocks):
    length = blocks * ROWS
    n1 = np.arange(blocks)[None, :]
    k1 = np.arange(blocks)[:, None] + 0.25
    n2 = np.arange(ROWS)[None, :]
    first = np.exp(-2j * np.pi * n1 * k1 / blocks)
    twist = np.exp(-2j * np.pi * n2 * k1 / length)
    second = np.exp(-2j * np.pi * n2 * n2.T / ROWS)
    first_high, first_low = split(np.concatenate([first.real, first.imag], 0))
    first_cat = np.concatenate([first_high, first_low], 1)
    wide = np.block([[second.real, second.imag], [-second.imag, second.real]])
    wide_high, wide_low = split(wide)
    last_high, last_low = split(np.concatenate([first.real, first.imag], 0).T / length)
    last_cat = np.concatenate([last_high, last_low, last_high], 1)
    twists = np.stack([twist.real, twist.imag]).astype(np.float32)
    return first_cat, twists, wide_high, wide_low, last_cat


def halves(value):
    high = value.astype(BF16)
    return high, (value - high.astype(F32)).astype(BF16)


def kernel(
    blocks, n_mp, model,
    gate_hbm, value_hbm, out_gate_hbm, taps_hbm, query_hbm, key_hbm, skip_hbm,
    first_hbm, twist_hbm, wide_high_hbm, wide_low_hbm, last_hbm,
    mixer_out, attended_out,
    gate_ref, value_ref, out_gate_ref, taps_ref, query_ref, skip_ref,
    first_ref, twist_ref, wide_high_ref, wide_low_ref, last_ref,
    send_taps, send_signal, send_gate, recv_taps, recv_signal, work, spectrum,
    gate_head, back_send, back_recv, key_all, value_row, value_old, value_all, probs, denoms,
    power_x, power_mp, scales,
    local_sems, send_sems, recv_sems,
):
    me = lax.axis_index("ctx")
    mp = lax.axis_index("mp")
    x, y = lax.rem(me, NX), lax.div(me, NX)
    n_y = blocks // NX
    width = NX * HEAD // blocks

    def far_first(k, count):
        half = lax.div(k + 1, 2)
        return lax.rem(count // 2 + jnp.where(lax.rem(k, 2) == 1, half, count - half), count)

    def ctx_peer(k):
        px = lax.rem(x + far_first(lax.rem(k, NX), NX), NX)
        py = lax.rem(y + far_first(lax.div(k, NX), n_y), n_y)
        return py * NX + px

    def mp_peer(k):
        return lax.rem(mp + far_first(k, n_mp), n_mp)

    barrier = pltpu.get_barrier_semaphore()

    def greet_ctx(k, carry):
        pl.semaphore_signal(barrier, inc=1, device_id={"ctx": ctx_peer(k)}, device_id_type=MESH)
        return carry

    def greet_mp(k, carry):
        pl.semaphore_signal(barrier, inc=1, device_id={"mp": mp_peer(k)}, device_id_type=MESH)
        return carry

    def fetch(src, dst, which):
        copy = pltpu.make_async_copy(src, dst, local_sems.at[which])
        copy.start()
        return copy

    first_loads = [
        fetch(src, dst, which)
        for which, (src, dst) in enumerate([(taps_hbm, taps_ref), (gate_hbm, gate_ref), (value_hbm, value_ref)])
    ]
    lax.fori_loop(0, blocks - 1, greet_ctx, 0)
    lax.fori_loop(0, n_mp - 1, greet_mp, 0)
    own_rows = pl.ds(SPAN * ROWS, ROWS)
    loads = [
        fetch(src, dst, 3 + which)
        for which, (src, dst) in enumerate([
            (out_gate_hbm, out_gate_ref), (first_hbm, first_ref), (twist_hbm, twist_ref),
            (wide_high_hbm, wide_high_ref), (wide_low_hbm, wide_low_ref), (last_hbm, last_ref), (skip_hbm, skip_ref),
            (query_hbm, query_ref), (key_hbm, key_all.at[own_rows]),
        ])
    ]

    def send(src, dst, which, target, send_which=None):
        pltpu.make_async_remote_copy(
            src_ref=src, dst_ref=dst, send_sem=send_sems.at[which if send_which is None else send_which],
            recv_sem=recv_sems.at[which], device_id=target, device_id_type=MESH,
        ).start()

    def received(ref, which):
        pltpu.make_async_copy(ref, ref, recv_sems.at[which]).wait()

    def sent(ref, which):
        pltpu.make_async_copy(ref, ref, send_sems.at[which]).wait()

    def group(d):
        return pl.ds(pl.multiple_of(lax.rem(d, NX) * HEAD + lax.div(d, NX) * width, width), width)

    mine = pl.ds(pl.multiple_of(me * width, width), width)
    my_lanes = pl.ds(pl.multiple_of(x * HEAD, HEAD), HEAD)

    first_loads[0].wait()
    send_taps[...] = taps_ref[...].T.astype(BF16)
    first_loads[1].wait()
    first_loads[2].wait()
    send_signal[...] = (gate_ref[...].astype(F32) * value_ref[...].astype(F32)).T.astype(BF16)
    pl.semaphore_wait(barrier, blocks - 1 + n_mp - 1)

    def spread(which, src, dst):
        def step(k, carry):
            d = ctx_peer(k)
            send(src.at[group(d)], dst.at[mine], which, {"ctx": d})
            return carry
        lax.fori_loop(0, blocks - 1, step, 0)
        dst[mine] = src[group(me)]

    spread(0, send_taps, recv_taps)
    spread(1, send_signal, recv_signal)

    loads[-1].wait()
    next_row = lax.rem(me + NX, blocks)
    own_keys, oldest_keys = key_all.at[own_rows], key_all.at[pl.ds(0, ROWS)]
    @pl.when(y < n_y - 1)
    def _():
        send(own_keys, oldest_keys, 3, {"ctx": next_row})

    for px in range(1, NX):
        @pl.when(x < px)
        def _():
            slot = pl.multiple_of((SPAN + x - px) * ROWS, ROWS)
            send(own_keys, key_all.at[pl.ds(slot, ROWS)], 4, {"ctx": y * NX + px})

    @pl.when(y == 0)
    def _():
        value_old[...] = jnp.zeros_like(value_old)
        power_x[pl.ds(0, NX)] = jnp.zeros((NX, 8, ROWS), F32)

    loads[0].wait()
    send_gate[...] = out_gate_ref[...].astype(F32).T.astype(BF16)
    for k in (2, 1, 3):
        px = lax.rem(x + k, NX)
        lanes = pl.ds(pl.multiple_of(px * HEAD, HEAD), HEAD)
        send(send_gate.at[lanes], gate_head.at[x], 2, {"ctx": y * NX + px})
    gate_head[x] = send_gate[my_lanes]

    for load in loads[1:-1]:
        load.wait()
    twist_real, twist_imag = twist_ref[0], twist_ref[1]

    def times_wide(value, contract):
        high, low = halves(value)
        dims = (((1,), (contract,)), ((), ()))

        def dot(a, b):
            return lax.dot_general(a, b, dims, preferred_element_type=F32)

        return dot(high, wide_high_ref[...]) + dot(low, wide_high_ref[...]) + dot(high, wide_low_ref[...])

    def lane_tile(value, c):
        return value[:, c * ROWS:(c + 1) * ROWS]

    def forward(recv):
        work[...] = recv[...].astype(F32)
        panel = jnp.concatenate([work[pl.ds(c, blocks, stride=width), :] for c in range(width)], 1).astype(BF16)
        panel = jnp.concatenate([panel, panel], 0)
        bins = jnp.dot(first_ref[...], panel, preferred_element_type=F32)
        real, imag = bins[:blocks], bins[blocks:]
        rows = []
        for c in range(width):
            a, b = lane_tile(real, c), lane_tile(imag, c)
            rows.append(jnp.concatenate([a * twist_real - b * twist_imag, a * twist_imag + b * twist_real], 1))
        return times_wide(jnp.concatenate(rows, 0), 0)

    remote_rows = pl.ds(0, (blocks - 1) * width)
    received(recv_taps.at[remote_rows], 0)
    spectrum[...] = forward(recv_taps)
    skip_at = x * HEAD + y * width
    for c in range(width):
        rows = pl.ds(c * blocks, blocks)
        spectrum[rows, pl.ds(0, ROWS)] = spectrum[rows, pl.ds(0, ROWS)] + skip_ref[skip_at + c]
    received(recv_signal.at[remote_rows], 1)

    bins = forward(recv_signal)
    a, b = bins[:, :ROWS], bins[:, ROWS:]
    c, d = spectrum[:, pl.ds(0, ROWS)], spectrum[:, pl.ds(ROWS, ROWS)]
    back = times_wide(jnp.concatenate([a * c - b * d, a * d + b * c], 1), 1)
    columns = []
    for c in range(width):
        part = back[c * blocks:(c + 1) * blocks]
        a, b = part[:, :ROWS], part[:, ROWS:]
        columns.append(jnp.concatenate([a * twist_real + b * twist_imag, b * twist_real - a * twist_imag], 0))
    high, low = halves(jnp.concatenate(columns, 1))
    convolved = jnp.dot(last_ref[...], jnp.concatenate([high, high, low], 0), preferred_element_type=F32)
    for c in range(width):
        work[pl.ds(c, blocks, stride=width), :] = lane_tile(convolved, c)
    back_send[...] = work[...].astype(BF16).reshape(blocks, width, ROWS)

    def send_back(k, carry):
        py = lax.rem(y + far_first(k, n_y), n_y)
        send(back_send.at[pl.ds(py * NX, NX)], back_recv.at[:, y], 5, {"ctx": py * NX + x})
        return carry

    lax.fori_loop(0, n_y - 1, send_back, 0)
    back_recv[:, y] = back_send[pl.ds(y * NX, NX)]

    @pl.when(y > 0)
    def _():
        received(oldest_keys, 3)

    for px in range(NX - 1):
        @pl.when(x > px)
        def _():
            slot = pl.multiple_of((x - px) * ROWS, ROWS)
            send(oldest_keys, key_all.at[pl.ds(slot, ROWS)], 4, {"ctx": y * NX + px})

    received(gate_head.at[pl.ds(0, NX - 1)], 2)
    received(back_send.at[pl.ds(0, (n_y - 1) * NX)], 5)
    gated = gate_head[...].astype(F32) * back_recv[...].reshape(NX, HEAD, ROWS).astype(F32)
    mixed = gated.astype(BF16)
    value_row[...] = mixed
    widened = mixed.astype(F32)
    power = jnp.sum(widened * widened, 1)
    power_x[NX + x] = jnp.concatenate([power, jnp.zeros_like(power)], 0)
    next_y = lax.rem(y + 1, n_y)
    for k in (2, 1, 3, 0):
        px = lax.rem(x + k, NX)

        @pl.when(y < n_y - 1)
        def _():
            send(power_x.at[NX + x], power_x.at[x], 7, {"ctx": next_y * NX + px})

        if k:
            send(power_x.at[NX + x], power_x.at[NX + x], 6, {"ctx": y * NX + px})

    @pl.when(y < n_y - 1)
    def _():
        send(value_row, value_old, 13, {"ctx": next_row}, 8)

    for px in range(NX):
        src, dst = value_row.at[pl.ds(0, px + 1)], value_all.at[pl.ds(SPAN - px, px + 1), x]

        @pl.when(x != px)
        def _():
            send(src, dst, 8 + x, {"ctx": y * NX + px}, 9 + px)

        @pl.when(x == px)
        def _():
            pltpu.make_async_copy(src, dst, recv_sems.at[8 + x]).start()

    received(power_x.at[pl.ds(0, NX - 1)], 6)

    @pl.when(y > 0)
    def _():
        received(power_x.at[pl.ds(0, NX)], 7)

    totals = []
    for half in range(2):
        total = power_x[half * NX]
        for k in range(1, NX):
            total = total + power_x[half * NX + k]
        totals.append(total[:NX])
    power_mp[mp] = jnp.concatenate(totals, 0)

    def share_power(k, carry):
        send(power_mp.at[mp], power_mp.at[mp], 12, {"mp": mp_peer(k)}, 13)
        return carry

    lax.fori_loop(0, n_mp - 1, share_power, 0)

    @pl.when(y > 0)
    def _():
        received(value_old, 13)

    for px in range(NX):
        src, dst = value_old.at[pl.ds(px, NX - px)], value_all.at[pl.ds(0, NX - px), x]

        @pl.when(x != px)
        def _():
            send(src, dst, 8 + x, {"ctx": y * NX + px}, 14 + px)

        @pl.when(x == px)
        def _():
            pltpu.make_async_copy(src, dst, recv_sems.at[8 + x]).start()

    received(key_all.at[pl.ds(0, (NX - 1) * ROWS)], 4)
    reach = (SPAN + 1) * ROWS
    key_at = lax.broadcasted_iota(jnp.int32, (reach, ROWS), 0)
    query_at = lax.broadcasted_iota(jnp.int32, (reach, ROWS), 1)
    first_key = jnp.maximum(SPAN - me, 0) * ROWS
    allowed = (key_at > query_at) & (key_at <= query_at + SPAN * ROWS) & (key_at >= first_key)
    for h in range(NX):
        lanes = pl.ds(h * HEAD, HEAD)
        scores = lax.dot_general(
            key_all[:, lanes], query_ref[:, lanes], (((1,), (1,)), ((), ())), preferred_element_type=F32
        ) * (1.0 / math.sqrt(HEAD))
        scores = jnp.where(allowed, scores, -1e30)
        weights = jnp.exp(scores - jnp.max(scores, 0, keepdims=True))
        denoms[h] = jnp.broadcast_to(jnp.sum(weights, 0, keepdims=True), (8, ROWS))
        probs[h] = weights.astype(BF16)

    for h in range(NX):
        received(value_all.at[:, h], 8 + h)
        mixer_out[:, pl.ds(h * HEAD, HEAD)] = value_all[SPAN, h].astype(F32).T.astype(BF16)

    received(power_mp.at[pl.ds(0, n_mp - 1)], 12)
    scales[...] = lax.rsqrt(jnp.sum(power_mp[...], 0) * (1.0 / model) + 1e-06)
    for h in range(NX):
        values = [
            (value_all[j, h].astype(F32) * scales[pl.ds(x + j, 1), :]).astype(BF16) for j in range(SPAN + 1)
        ]
        summed = jnp.dot(jnp.concatenate(values, 1), probs[h], preferred_element_type=F32)
        attended_out[:, pl.ds(h * HEAD, HEAD)] = (summed / denoms[h][0:1]).T.astype(BF16)

    sent(recv_taps.at[remote_rows], 0)
    sent(recv_signal.at[remote_rows], 1)
    sent(gate_head.at[pl.ds(0, NX - 1)], 2)
    @pl.when(y < n_y - 1)
    def _():
        sent(oldest_keys, 3)
        sent(power_x.at[pl.ds(0, NX)], 7)
        sent(value_row, 8)

    sent(key_all.at[pl.ds(0, (NX - 1) * ROWS)], 4)
    sent(back_send.at[pl.ds(0, (n_y - 1) * NX)], 5)
    sent(power_x.at[pl.ds(0, NX - 1)], 6)
    for px in range(NX):
        @pl.when(x != px)
        def _():
            sent(value_row.at[pl.ds(0, px + 1)], 9 + px)
            sent(value_row.at[pl.ds(0, NX - px)], 14 + px)
    sent(power_mp.at[pl.ds(0, n_mp - 1)], 13)


def hand_over(mixer_from, attended_from, mixer_to, attended_to, sems):
    copies = [
        pltpu.make_async_copy(mixer_from, mixer_to, sems.at[0]),
        pltpu.make_async_copy(attended_from, attended_to, sems.at[1]),
    ]
    for copy in copies:
        copy.start()
    for copy in copies:
        copy.wait()


def solution(mesh):
    blocks, n_mp = mesh.shape["ctx"], mesh.shape["mp"]
    constants = tables(blocks)

    def local(gate_in, value_in, gate_out, filter_taps, skip_gain, queries, key_rows):
        rows, lanes = gate_in.shape
        width = lanes // blocks
        n_y = blocks // NX
        hbm = pl.BlockSpec(memory_space=pltpu.HBM)
        square = (NX, ROWS, HEAD)
        operands = gate_in, value_in, gate_out, filter_taps, queries, key_rows, skip_gain, *constants
        operands = [pltpu.with_memory_space_constraint(o, pltpu.HBM) for o in operands]
        mixer, attended = pl.pallas_call(
            functools.partial(kernel, blocks, n_mp, n_mp * lanes),
            out_shape=(pltpu.VMEM((rows, lanes), BF16),) * 2,
            in_specs=[hbm] * 12,
            out_specs=(pl.BlockSpec(memory_space=pltpu.VMEM),) * 2,
            scratch_shapes=[
                *(pltpu.VMEM((rows, lanes), BF16),) * 3,
                pltpu.VMEM((rows, lanes), F32),
                pltpu.VMEM((rows, lanes), BF16),
                pltpu.SMEM((lanes,), F32),
                *(pltpu.VMEM(c.shape, c.dtype) for c in constants),
                *(pltpu.VMEM((lanes, ROWS), BF16),) * 5,
                pltpu.VMEM((lanes, ROWS), F32),
                pltpu.VMEM((lanes, 2 * ROWS), F32),
                pltpu.VMEM(square, BF16),
                pltpu.VMEM((blocks, width, ROWS), BF16),
                pltpu.VMEM((NX, n_y, width, ROWS), BF16),
                pltpu.VMEM(((SPAN + 1) * ROWS, lanes), BF16),
                pltpu.VMEM(square, BF16),
                pltpu.VMEM(square, BF16),
                pltpu.VMEM((SPAN + 1, NX, HEAD, ROWS), BF16),
                pltpu.VMEM((NX, (SPAN + 1) * ROWS, ROWS), BF16),
                pltpu.VMEM((NX, 8, ROWS), F32),
                pltpu.VMEM((2 * NX, 8, ROWS), F32),
                pltpu.VMEM((n_mp, 8, ROWS), F32),
                pltpu.VMEM((8, ROWS), F32),
                pltpu.SemaphoreType.DMA((14,)),
                pltpu.SemaphoreType.DMA((18,)),
                pltpu.SemaphoreType.DMA((14,)),
            ],
            compiler_params=pltpu.CompilerParams(
                collective_id=0, has_side_effects=True, vmem_limit_bytes=32 * 2**20
            ),
            cost_estimate=pl.CostEstimate(flops=2 * 10**9, bytes_accessed=2 * 10**6, transcendentals=4 * 10**5),
        )(*operands)
        return pl.pallas_call(
            hand_over,
            out_shape=(jax.ShapeDtypeStruct((rows, lanes), BF16),) * 2,
            in_specs=[pl.BlockSpec(memory_space=pltpu.VMEM)] * 2,
            out_specs=(hbm,) * 2,
            scratch_shapes=[pltpu.SemaphoreType.DMA((2,))],
            compiler_params=pltpu.CompilerParams(vmem_limit_bytes=8 * 2**20),
        )(mixer, attended)

    return jax.shard_map(
        local,
        mesh=mesh,
        in_specs=(P("ctx", "mp"),) * 4 + (P("mp"),) + (P("ctx", "mp"),) * 2,
        out_specs=(P("ctx", "mp"), P("ctx", "mp")),
        check_vma=False,
    )
```

```python
import functools
import math

import jax
import jax.numpy as jnp
import ml_dtypes
import numpy as np
from jax import lax
from jax.experimental import pallas as pl
from jax.experimental.pallas import tpu as pltpu
from jax.sharding import PartitionSpec as P

HEAD = 128
ROWS = 128
SPAN = 4
NX = 4
MESH = pl.DeviceIdType.MESH
F32 = jnp.float32
BF16 = jnp.bfloat16


def split(table):
    high = table.astype(np.float32).astype(ml_dtypes.bfloat16)
    low = (table - high.astype(np.float64)).astype(np.float32).astype(ml_dtypes.bfloat16)
    return high, low


def tables(blocks):
    length = blocks * ROWS
    n1 = np.arange(blocks)[None, :]
    k1 = np.arange(blocks)[:, None] + 0.25
    n2 = np.arange(ROWS)[None, :]
    first = np.exp(-2j * np.pi * n1 * k1 / blocks)
    twist = np.exp(-2j * np.pi * n2 * k1 / length)
    second = np.exp(-2j * np.pi * n2 * n2.T / ROWS)
    first_high, first_low = split(np.concatenate([first.real, first.imag], 0))
    first_cat = np.concatenate([first_high, first_low], 1)
    wide = np.block([[second.real, second.imag], [-second.imag, second.real]])
    wide_high, wide_low = split(wide)
    last_high, last_low = split(np.concatenate([first.real, first.imag], 0).T / length)
    last_cat = np.concatenate([last_high, last_low, last_high], 1)
    twists = np.stack([twist.real, twist.imag]).astype(np.float32)
    return first_cat, twists, wide_high, wide_low, last_cat


def halves(value):
    high = value.astype(BF16)
    return high, (value - high.astype(F32)).astype(BF16)


def kernel(
    blocks, n_mp, model,
    gate_hbm, value_hbm, out_gate_hbm, taps_hbm, query_hbm, key_hbm, skip_hbm,
    first_hbm, twist_hbm, wide_high_hbm, wide_low_hbm, last_hbm,
    mixer_out, value_all, probs, denoms, scales,
    gate_ref, value_ref, out_gate_ref, taps_ref, query_ref, skip_ref,
    first_ref, twist_ref, wide_high_ref, wide_low_ref, last_ref,
    send_taps, send_signal, send_gate, recv_taps, recv_signal, work, spectrum,
    gate_head, back_send, back_recv, key_all, value_row, value_old,
    power_x, power_mp,
    local_sems, send_sems, recv_sems,
):
    me = lax.axis_index("ctx")
    mp = lax.axis_index("mp")
    x, y = lax.rem(me, NX), lax.div(me, NX)
    n_y = blocks // NX
    width = NX * HEAD // blocks

    def far_first(k, count):
        half = lax.div(k + 1, 2)
        return lax.rem(count // 2 + jnp.where(lax.rem(k, 2) == 1, half, count - half), count)

    def ctx_peer(k):
        px = lax.rem(x + far_first(lax.rem(k, NX), NX), NX)
        py = lax.rem(y + far_first(lax.div(k, NX), n_y), n_y)
        return py * NX + px

    def mp_peer(k):
        return lax.rem(mp + far_first(k, n_mp), n_mp)

    barrier = pltpu.get_barrier_semaphore()

    def greet_ctx(k, carry):
        pl.semaphore_signal(barrier, inc=1, device_id={"ctx": ctx_peer(k)}, device_id_type=MESH)
        return carry

    def greet_mp(k, carry):
        pl.semaphore_signal(barrier, inc=1, device_id={"mp": mp_peer(k)}, device_id_type=MESH)
        return carry

    def fetch(src, dst, which):
        copy = pltpu.make_async_copy(src, dst, local_sems.at[which])
        copy.start()
        return copy

    first_loads = [
        fetch(src, dst, which)
        for which, (src, dst) in enumerate([(taps_hbm, taps_ref), (gate_hbm, gate_ref), (value_hbm, value_ref)])
    ]
    lax.fori_loop(0, blocks - 1, greet_ctx, 0)
    lax.fori_loop(0, n_mp - 1, greet_mp, 0)
    own_rows = pl.ds(SPAN * ROWS, ROWS)
    loads = [
        fetch(src, dst, 3 + which)
        for which, (src, dst) in enumerate([
            (out_gate_hbm, out_gate_ref), (first_hbm, first_ref), (twist_hbm, twist_ref),
            (wide_high_hbm, wide_high_ref), (wide_low_hbm, wide_low_ref), (last_hbm, last_ref), (skip_hbm, skip_ref),
            (query_hbm, query_ref), (key_hbm, key_all.at[own_rows]),
        ])
    ]

    def send(src, dst, which, target, send_which=None):
        pltpu.make_async_remote_copy(
            src_ref=src, dst_ref=dst, send_sem=send_sems.at[which if send_which is None else send_which],
            recv_sem=recv_sems.at[which], device_id=target, device_id_type=MESH,
        ).start()

    def received(ref, which):
        pltpu.make_async_copy(ref, ref, recv_sems.at[which]).wait()

    def sent(ref, which):
        pltpu.make_async_copy(ref, ref, send_sems.at[which]).wait()

    def group(d):
        return pl.ds(pl.multiple_of(lax.rem(d, NX) * HEAD + lax.div(d, NX) * width, width), width)

    mine = pl.ds(pl.multiple_of(me * width, width), width)
    my_lanes = pl.ds(pl.multiple_of(x * HEAD, HEAD), HEAD)

    first_loads[0].wait()
    send_taps[...] = taps_ref[...].T.astype(BF16)
    first_loads[1].wait()
    first_loads[2].wait()
    send_signal[...] = (gate_ref[...].astype(F32) * value_ref[...].astype(F32)).T.astype(BF16)
    pl.semaphore_wait(barrier, blocks - 1 + n_mp - 1)

    def spread(which, src, dst):
        def step(k, carry):
            d = ctx_peer(k)
            send(src.at[group(d)], dst.at[mine], which, {"ctx": d})
            return carry
        lax.fori_loop(0, blocks - 1, step, 0)
        dst[mine] = src[group(me)]

    spread(0, send_taps, recv_taps)
    spread(1, send_signal, recv_signal)

    loads[-1].wait()
    next_row = lax.rem(me + NX, blocks)
    own_keys, oldest_keys = key_all.at[own_rows], key_all.at[pl.ds(0, ROWS)]
    @pl.when(y < n_y - 1)
    def _():
        send(own_keys, oldest_keys, 3, {"ctx": next_row})

    for px in range(1, NX):
        @pl.when(x < px)
        def _():
            slot = pl.multiple_of((SPAN + x - px) * ROWS, ROWS)
            send(own_keys, key_all.at[pl.ds(slot, ROWS)], 4, {"ctx": y * NX + px})

    @pl.when(y == 0)
    def _():
        value_old[...] = jnp.zeros_like(value_old)
        power_x[pl.ds(0, NX)] = jnp.zeros((NX, 8, ROWS), F32)

    loads[0].wait()
    send_gate[...] = out_gate_ref[...].astype(F32).T.astype(BF16)
    for k in (2, 1, 3):
        px = lax.rem(x + k, NX)
        lanes = pl.ds(pl.multiple_of(px * HEAD, HEAD), HEAD)
        send(send_gate.at[lanes], gate_head.at[x], 2, {"ctx": y * NX + px})
    gate_head[x] = send_gate[my_lanes]

    for load in loads[1:-1]:
        load.wait()
    twist_real, twist_imag = twist_ref[0], twist_ref[1]

    def times_wide(value, contract):
        high, low = halves(value)
        dims = (((1,), (contract,)), ((), ()))

        def dot(a, b):
            return lax.dot_general(a, b, dims, preferred_element_type=F32)

        return dot(high, wide_high_ref[...]) + dot(low, wide_high_ref[...]) + dot(high, wide_low_ref[...])

    def lane_tile(value, c):
        return value[:, c * ROWS:(c + 1) * ROWS]

    def forward(recv):
        work[...] = recv[...].astype(F32)
        panel = jnp.concatenate([work[pl.ds(c, blocks, stride=width), :] for c in range(width)], 1).astype(BF16)
        panel = jnp.concatenate([panel, panel], 0)
        bins = jnp.dot(first_ref[...], panel, preferred_element_type=F32)
        real, imag = bins[:blocks], bins[blocks:]
        rows = []
        for c in range(width):
            a, b = lane_tile(real, c), lane_tile(imag, c)
            rows.append(jnp.concatenate([a * twist_real - b * twist_imag, a * twist_imag + b * twist_real], 1))
        return times_wide(jnp.concatenate(rows, 0), 0)

    remote_rows = pl.ds(0, (blocks - 1) * width)
    received(recv_taps.at[remote_rows], 0)
    spectrum[...] = forward(recv_taps)
    skip_at = x * HEAD + y * width
    for c in range(width):
        rows = pl.ds(c * blocks, blocks)
        spectrum[rows, pl.ds(0, ROWS)] = spectrum[rows, pl.ds(0, ROWS)] + skip_ref[skip_at + c]
    received(recv_signal.at[remote_rows], 1)

    bins = forward(recv_signal)
    a, b = bins[:, :ROWS], bins[:, ROWS:]
    c, d = spectrum[:, pl.ds(0, ROWS)], spectrum[:, pl.ds(ROWS, ROWS)]
    back = times_wide(jnp.concatenate([a * c - b * d, a * d + b * c], 1), 1)
    columns = []
    for c in range(width):
        part = back[c * blocks:(c + 1) * blocks]
        a, b = part[:, :ROWS], part[:, ROWS:]
        columns.append(jnp.concatenate([a * twist_real + b * twist_imag, b * twist_real - a * twist_imag], 0))
    high, low = halves(jnp.concatenate(columns, 1))
    convolved = jnp.dot(last_ref[...], jnp.concatenate([high, high, low], 0), preferred_element_type=F32)
    for c in range(width):
        work[pl.ds(c, blocks, stride=width), :] = lane_tile(convolved, c)
    back_send[...] = work[...].astype(BF16).reshape(blocks, width, ROWS)

    def send_back(k, carry):
        py = lax.rem(y + far_first(k, n_y), n_y)
        send(back_send.at[pl.ds(py * NX, NX)], back_recv.at[:, y], 5, {"ctx": py * NX + x})
        return carry

    lax.fori_loop(0, n_y - 1, send_back, 0)
    back_recv[:, y] = back_send[pl.ds(y * NX, NX)]

    @pl.when(y > 0)
    def _():
        received(oldest_keys, 3)

    for px in range(NX - 1):
        @pl.when(x > px)
        def _():
            slot = pl.multiple_of((x - px) * ROWS, ROWS)
            send(oldest_keys, key_all.at[pl.ds(slot, ROWS)], 4, {"ctx": y * NX + px})

    received(gate_head.at[pl.ds(0, NX - 1)], 2)
    received(back_send.at[pl.ds(0, (n_y - 1) * NX)], 5)
    gated = gate_head[...].astype(F32) * back_recv[...].reshape(NX, HEAD, ROWS).astype(F32)
    mixed = gated.astype(BF16)
    value_row[...] = mixed
    widened = mixed.astype(F32)
    power = jnp.sum(widened * widened, 1)
    power_x[NX + x] = jnp.concatenate([power, jnp.zeros_like(power)], 0)
    next_y = lax.rem(y + 1, n_y)
    for k in (2, 1, 3, 0):
        px = lax.rem(x + k, NX)

        @pl.when(y < n_y - 1)
        def _():
            send(power_x.at[NX + x], power_x.at[x], 7, {"ctx": next_y * NX + px})

        if k:
            send(power_x.at[NX + x], power_x.at[NX + x], 6, {"ctx": y * NX + px})

    @pl.when(y < n_y - 1)
    def _():
        send(value_row, value_old, 13, {"ctx": next_row}, 8)

    for px in range(NX):
        src, dst = value_row.at[pl.ds(0, px + 1)], value_all.at[pl.ds(SPAN - px, px + 1), x]

        @pl.when(x != px)
        def _():
            send(src, dst, 8 + x, {"ctx": y * NX + px}, 9 + px)

        @pl.when(x == px)
        def _():
            pltpu.make_async_copy(src, dst, recv_sems.at[8 + x]).start()

    received(power_x.at[pl.ds(0, NX - 1)], 6)

    @pl.when(y > 0)
    def _():
        received(power_x.at[pl.ds(0, NX)], 7)

    totals = []
    for half in range(2):
        total = power_x[half * NX]
        for k in range(1, NX):
            total = total + power_x[half * NX + k]
        totals.append(total[:NX])
    power_mp[mp] = jnp.concatenate(totals, 0)

    def share_power(k, carry):
        send(power_mp.at[mp], power_mp.at[mp], 12, {"mp": mp_peer(k)}, 13)
        return carry

    lax.fori_loop(0, n_mp - 1, share_power, 0)

    @pl.when(y > 0)
    def _():
        received(value_old, 13)

    for px in range(NX):
        src, dst = value_old.at[pl.ds(px, NX - px)], value_all.at[pl.ds(0, NX - px), x]

        @pl.when(x != px)
        def _():
            send(src, dst, 8 + x, {"ctx": y * NX + px}, 14 + px)

        @pl.when(x == px)
        def _():
            pltpu.make_async_copy(src, dst, recv_sems.at[8 + x]).start()

    received(key_all.at[pl.ds(0, (NX - 1) * ROWS)], 4)
    reach = (SPAN + 1) * ROWS
    key_at = lax.broadcasted_iota(jnp.int32, (reach, ROWS), 0)
    query_at = lax.broadcasted_iota(jnp.int32, (reach, ROWS), 1)
    first_key = jnp.maximum(SPAN - me, 0) * ROWS
    allowed = (key_at > query_at) & (key_at <= query_at + SPAN * ROWS) & (key_at >= first_key)
    for h in range(NX):
        lanes = pl.ds(h * HEAD, HEAD)
        scores = lax.dot_general(
            key_all[:, lanes], query_ref[:, lanes], (((1,), (1,)), ((), ())), preferred_element_type=F32
        ) * (1.0 / math.sqrt(HEAD))
        scores = jnp.where(allowed, scores, -1e30)
        weights = jnp.exp(scores - jnp.max(scores, 0, keepdims=True))
        denoms[h] = jnp.broadcast_to(jnp.sum(weights, 0, keepdims=True), (8, ROWS))
        probs[h] = weights.astype(BF16)

    for h in range(NX):
        received(value_all.at[:, h], 8 + h)
        mixer_out[:, pl.ds(h * HEAD, HEAD)] = value_all[SPAN, h].astype(F32).T.astype(BF16)

    received(power_mp.at[pl.ds(0, n_mp - 1)], 12)
    scales[...] = lax.rsqrt(jnp.sum(power_mp[...], 0) * (1.0 / model) + 1e-06)

    sent(recv_taps.at[remote_rows], 0)
    sent(recv_signal.at[remote_rows], 1)
    sent(gate_head.at[pl.ds(0, NX - 1)], 2)
    @pl.when(y < n_y - 1)
    def _():
        sent(oldest_keys, 3)
        sent(power_x.at[pl.ds(0, NX)], 7)
        sent(value_row, 8)

    sent(key_all.at[pl.ds(0, (NX - 1) * ROWS)], 4)
    sent(back_send.at[pl.ds(0, (n_y - 1) * NX)], 5)
    sent(power_x.at[pl.ds(0, NX - 1)], 6)
    for px in range(NX):
        @pl.when(x != px)
        def _():
            sent(value_row.at[pl.ds(0, px + 1)], 9 + px)
            sent(value_row.at[pl.ds(0, NX - px)], 14 + px)
    sent(power_mp.at[pl.ds(0, n_mp - 1)], 13)


def attend(mixer_from, value_all, probs, denoms, scales, mixer_to, attended_to, attended, sems):
    x = lax.rem(lax.axis_index("ctx"), NX)
    copies = [pltpu.make_async_copy(mixer_from, mixer_to, sems.at[NX])]
    copies[0].start()
    for h in range(NX):
        values = [
            (value_all[j, h].astype(F32) * scales[pl.ds(x + j, 1), :]).astype(BF16) for j in range(SPAN + 1)
        ]
        summed = jnp.dot(jnp.concatenate(values, 1), probs[h], preferred_element_type=F32)
        lanes = pl.ds(h * HEAD, HEAD)
        attended[:, lanes] = (summed / denoms[h][0:1]).T.astype(BF16)
        copies.append(pltpu.make_async_copy(attended.at[:, lanes], attended_to.at[:, lanes], sems.at[h]))
        copies[-1].start()
    for copy in copies:
        copy.wait()


def solution(mesh):
    blocks, n_mp = mesh.shape["ctx"], mesh.shape["mp"]
    constants = tables(blocks)

    def local(gate_in, value_in, gate_out, filter_taps, skip_gain, queries, key_rows):
        rows, lanes = gate_in.shape
        width = lanes // blocks
        n_y = blocks // NX
        hbm = pl.BlockSpec(memory_space=pltpu.HBM)
        square = (NX, ROWS, HEAD)
        operands = gate_in, value_in, gate_out, filter_taps, queries, key_rows, skip_gain, *constants
        operands = [pltpu.with_memory_space_constraint(o, pltpu.HBM) for o in operands]
        held = pl.pallas_call(
            functools.partial(kernel, blocks, n_mp, n_mp * lanes),
            out_shape=(
                pltpu.VMEM((rows, lanes), BF16),
                pltpu.VMEM((SPAN + 1, NX, HEAD, ROWS), BF16),
                pltpu.VMEM((NX, (SPAN + 1) * ROWS, ROWS), BF16),
                pltpu.VMEM((NX, 8, ROWS), F32),
                pltpu.VMEM((8, ROWS), F32),
            ),
            in_specs=[hbm] * 12,
            out_specs=(pl.BlockSpec(memory_space=pltpu.VMEM),) * 5,
            scratch_shapes=[
                *(pltpu.VMEM((rows, lanes), BF16),) * 3,
                pltpu.VMEM((rows, lanes), F32),
                pltpu.VMEM((rows, lanes), BF16),
                pltpu.SMEM((lanes,), F32),
                *(pltpu.VMEM(c.shape, c.dtype) for c in constants),
                *(pltpu.VMEM((lanes, ROWS), BF16),) * 5,
                pltpu.VMEM((lanes, ROWS), F32),
                pltpu.VMEM((lanes, 2 * ROWS), F32),
                pltpu.VMEM(square, BF16),
                pltpu.VMEM((blocks, width, ROWS), BF16),
                pltpu.VMEM((NX, n_y, width, ROWS), BF16),
                pltpu.VMEM(((SPAN + 1) * ROWS, lanes), BF16),
                pltpu.VMEM(square, BF16),
                pltpu.VMEM(square, BF16),
                pltpu.VMEM((2 * NX, 8, ROWS), F32),
                pltpu.VMEM((n_mp, 8, ROWS), F32),
                pltpu.SemaphoreType.DMA((14,)),
                pltpu.SemaphoreType.DMA((18,)),
                pltpu.SemaphoreType.DMA((14,)),
            ],
            compiler_params=pltpu.CompilerParams(
                collective_id=0, has_side_effects=True, vmem_limit_bytes=32 * 2**20
            ),
            cost_estimate=pl.CostEstimate(flops=2 * 10**9, bytes_accessed=2 * 10**6, transcendentals=4 * 10**5),
        )(*operands)
        return pl.pallas_call(
            attend,
            out_shape=(jax.ShapeDtypeStruct((rows, lanes), BF16),) * 2,
            in_specs=[pl.BlockSpec(memory_space=pltpu.VMEM)] * 5,
            out_specs=(hbm,) * 2,
            scratch_shapes=[pltpu.VMEM((rows, lanes), BF16), pltpu.SemaphoreType.DMA((NX + 1,))],
            compiler_params=pltpu.CompilerParams(vmem_limit_bytes=8 * 2**20),
        )(*held)

    return jax.shard_map(
        local,
        mesh=mesh,
        in_specs=(P("ctx", "mp"),) * 4 + (P("mp"),) + (P("ctx", "mp"),) * 2,
        out_specs=(P("ctx", "mp"), P("ctx", "mp")),
        check_vma=False,
    )
```

```python
import functools
import math

import jax
import jax.numpy as jnp
import ml_dtypes
import numpy as np
from jax import lax
from jax.experimental import pallas as pl
from jax.experimental.pallas import tpu as pltpu
from jax.sharding import PartitionSpec as P

HEAD = 128
ROWS = 128
SPAN = 4
NX = 4
MESH = pl.DeviceIdType.MESH
F32 = jnp.float32
BF16 = jnp.bfloat16


def split(table):
    high = table.astype(np.float32).astype(ml_dtypes.bfloat16)
    low = (table - high.astype(np.float64)).astype(np.float32).astype(ml_dtypes.bfloat16)
    return high, low


def tables(blocks):
    length = blocks * ROWS
    n1 = np.arange(blocks)[None, :]
    k1 = np.arange(blocks)[:, None] + 0.25
    n2 = np.arange(ROWS)[None, :]
    first = np.exp(-2j * np.pi * n1 * k1 / blocks)
    twist = np.exp(-2j * np.pi * n2 * k1 / length)
    second = np.exp(-2j * np.pi * n2 * n2.T / ROWS)
    first_high, first_low = split(np.concatenate([first.real, first.imag], 0))
    first_cat = np.concatenate([first_high, first_low], 1)
    wide = np.block([[second.real, second.imag], [-second.imag, second.real]])
    wide_high, wide_low = split(wide)
    last_high, last_low = split(np.concatenate([first.real, first.imag], 0).T / length)
    last_cat = np.concatenate([last_high, last_low, last_high], 1)
    twists = np.stack([twist.real, twist.imag]).astype(np.float32)
    return first_cat, twists, wide_high, wide_low, last_cat


def halves(value):
    high = value.astype(BF16)
    return high, (value - high.astype(F32)).astype(BF16)


def kernel(
    blocks, n_mp, model,
    gate_hbm, value_hbm, out_gate_hbm, taps_hbm, query_hbm, key_hbm, skip_hbm,
    first_hbm, twist_hbm, wide_high_hbm, wide_low_hbm, last_hbm,
    mixer_out, value_all, probs, denoms, scales,
    gate_ref, value_ref, out_gate_ref, taps_ref, query_ref, skip_ref,
    first_ref, twist_ref, wide_high_ref, wide_low_ref, last_ref,
    send_taps, send_signal, send_gate, recv_taps, recv_signal, work, spectrum,
    gate_head, back_send, back_recv, key_all, value_row, value_old,
    power_x, power_mp,
    local_sems, send_sems, recv_sems,
):
    me = lax.axis_index("ctx")
    mp = lax.axis_index("mp")
    x, y = lax.rem(me, NX), lax.div(me, NX)
    n_y = blocks // NX
    width = NX * HEAD // blocks

    def far_first(k, count):
        half = lax.div(k + 1, 2)
        return lax.rem(count // 2 + jnp.where(lax.rem(k, 2) == 1, half, count - half), count)

    def ctx_peer(k):
        px = lax.rem(x + far_first(lax.rem(k, NX), NX), NX)
        py = lax.rem(y + far_first(lax.div(k, NX), n_y), n_y)
        return py * NX + px

    def mp_peer(k):
        return lax.rem(mp + far_first(k, n_mp), n_mp)

    barrier = pltpu.get_barrier_semaphore()

    def greet_ctx(k, carry):
        pl.semaphore_signal(barrier, inc=1, device_id={"ctx": ctx_peer(k)}, device_id_type=MESH)
        return carry

    def greet_mp(k, carry):
        pl.semaphore_signal(barrier, inc=1, device_id={"mp": mp_peer(k)}, device_id_type=MESH)
        return carry

    def fetch(src, dst, which):
        copy = pltpu.make_async_copy(src, dst, local_sems.at[which])
        copy.start()
        return copy

    first_loads = [
        fetch(src, dst, which)
        for which, (src, dst) in enumerate([(taps_hbm, taps_ref), (gate_hbm, gate_ref), (value_hbm, value_ref)])
    ]
    lax.fori_loop(0, blocks - 1, greet_ctx, 0)
    lax.fori_loop(0, n_mp - 1, greet_mp, 0)
    own_rows = pl.ds(SPAN * ROWS, ROWS)
    loads = [
        fetch(src, dst, 3 + which)
        for which, (src, dst) in enumerate([
            (out_gate_hbm, out_gate_ref), (first_hbm, first_ref), (twist_hbm, twist_ref),
            (wide_high_hbm, wide_high_ref), (wide_low_hbm, wide_low_ref), (last_hbm, last_ref), (skip_hbm, skip_ref),
            (query_hbm, query_ref), (key_hbm, key_all.at[own_rows]),
        ])
    ]

    def send(src, dst, which, target, send_which=None):
        pltpu.make_async_remote_copy(
            src_ref=src, dst_ref=dst, send_sem=send_sems.at[which if send_which is None else send_which],
            recv_sem=recv_sems.at[which], device_id=target, device_id_type=MESH,
        ).start()

    def received(ref, which):
        pltpu.make_async_copy(ref, ref, recv_sems.at[which]).wait()

    def sent(ref, which):
        pltpu.make_async_copy(ref, ref, send_sems.at[which]).wait()

    def group(d):
        return pl.ds(pl.multiple_of(lax.rem(d, NX) * HEAD + lax.div(d, NX) * width, width), width)

    mine = pl.ds(pl.multiple_of(me * width, width), width)
    my_lanes = pl.ds(pl.multiple_of(x * HEAD, HEAD), HEAD)

    first_loads[0].wait()
    send_taps[...] = taps_ref[...].T.astype(BF16)
    first_loads[1].wait()
    first_loads[2].wait()
    send_signal[...] = (gate_ref[...].astype(F32) * value_ref[...].astype(F32)).T.astype(BF16)
    pl.semaphore_wait(barrier, blocks - 1 + n_mp - 1)

    def spread(which, src, dst):
        def step(k, carry):
            d = ctx_peer(k)
            send(src.at[group(d)], dst.at[mine], which, {"ctx": d})
            return carry
        lax.fori_loop(0, blocks - 1, step, 0)
        dst[mine] = src[group(me)]

    spread(0, send_taps, recv_taps)
    spread(1, send_signal, recv_signal)

    loads[-1].wait()
    next_row = lax.rem(me + NX, blocks)
    own_keys, oldest_keys = key_all.at[own_rows], key_all.at[pl.ds(0, ROWS)]
    @pl.when(y < n_y - 1)
    def _():
        send(own_keys, oldest_keys, 3, {"ctx": next_row})

    for px in range(1, NX):
        @pl.when(x < px)
        def _():
            slot = pl.multiple_of((SPAN + x - px) * ROWS, ROWS)
            send(own_keys, key_all.at[pl.ds(slot, ROWS)], 4, {"ctx": y * NX + px})

    @pl.when(y == 0)
    def _():
        value_old[...] = jnp.zeros_like(value_old)
        power_x[pl.ds(0, NX)] = jnp.zeros((NX, 8, ROWS), F32)

    loads[0].wait()
    send_gate[...] = out_gate_ref[...].astype(F32).T.astype(BF16)
    for k in (2, 1, 3):
        px = lax.rem(x + k, NX)
        lanes = pl.ds(pl.multiple_of(px * HEAD, HEAD), HEAD)
        send(send_gate.at[lanes], gate_head.at[x], 2, {"ctx": y * NX + px})
    gate_head[x] = send_gate[my_lanes]

    for load in loads[1:-1]:
        load.wait()
    twist_real, twist_imag = twist_ref[0], twist_ref[1]

    def times_wide(value, contract):
        high, low = halves(value)
        dims = (((1,), (contract,)), ((), ()))

        def dot(a, b):
            return lax.dot_general(a, b, dims, preferred_element_type=F32)

        return dot(high, wide_high_ref[...]) + dot(low, wide_high_ref[...]) + dot(high, wide_low_ref[...])

    def lane_tile(value, c):
        return value[:, c * ROWS:(c + 1) * ROWS]

    def forward(recv):
        work[all_rows] = recv[...].astype(F32)
        panel = jnp.concatenate([work[pl.ds(c, blocks, stride=width), :] for c in range(width)], 1).astype(BF16)
        panel = jnp.concatenate([panel, panel], 0)
        bins = jnp.dot(first_ref[...], panel, preferred_element_type=F32)
        real, imag = bins[:blocks], bins[blocks:]
        rows = []
        for c in range(width):
            a, b = lane_tile(real, c), lane_tile(imag, c)
            rows.append(jnp.concatenate([a * twist_real - b * twist_imag, a * twist_imag + b * twist_real], 1))
        return times_wide(jnp.concatenate(rows, 0), 0)

    remote_rows, all_rows = pl.ds(0, (blocks - 1) * width), pl.ds(0, blocks * width)
    received(recv_taps.at[remote_rows], 0)
    spectrum[...] = forward(recv_taps)
    skip_at = x * HEAD + y * width
    for c in range(width):
        rows = pl.ds(c * blocks, blocks)
        spectrum[rows, pl.ds(0, ROWS)] = spectrum[rows, pl.ds(0, ROWS)] + skip_ref[skip_at + c]
    received(recv_signal.at[remote_rows], 1)

    bins = forward(recv_signal)
    a, b = bins[:, :ROWS], bins[:, ROWS:]
    c, d = spectrum[:, pl.ds(0, ROWS)], spectrum[:, pl.ds(ROWS, ROWS)]
    back = times_wide(jnp.concatenate([a * c - b * d, a * d + b * c], 1), 1)
    columns = []
    for c in range(width):
        part = back[c * blocks:(c + 1) * blocks]
        a, b = part[:, :ROWS], part[:, ROWS:]
        columns.append(jnp.concatenate([a * twist_real + b * twist_imag, b * twist_real - a * twist_imag], 0))
    high, low = halves(jnp.concatenate(columns, 1))
    convolved = jnp.dot(last_ref[...], jnp.concatenate([high, high, low], 0), preferred_element_type=F32)
    for c in range(width):
        work[pl.ds(c, blocks, stride=width), :] = lane_tile(convolved, c)
    back_send[...] = work[all_rows].astype(BF16).reshape(blocks, width, ROWS)

    def send_back(k, carry):
        py = lax.rem(y + far_first(k, n_y), n_y)
        send(back_send.at[pl.ds(py * NX, NX)], back_recv.at[:, y], 5, {"ctx": py * NX + x})
        return carry

    lax.fori_loop(0, n_y - 1, send_back, 0)
    back_recv[:, y] = back_send[pl.ds(y * NX, NX)]

    @pl.when(y > 0)
    def _():
        received(oldest_keys, 3)

    for px in range(NX - 1):
        @pl.when(x > px)
        def _():
            slot = pl.multiple_of((x - px) * ROWS, ROWS)
            send(oldest_keys, key_all.at[pl.ds(slot, ROWS)], 4, {"ctx": y * NX + px})

    received(gate_head.at[pl.ds(0, NX - 1)], 2)
    received(back_send.at[pl.ds(0, (n_y - 1) * NX)], 5)
    gated = gate_head[...].astype(F32) * back_recv[...].reshape(NX, HEAD, ROWS).astype(F32)
    mixed = gated.astype(BF16)
    value_row[...] = mixed
    widened = mixed.astype(F32)
    power = jnp.sum(widened * widened, 1)
    power_x[NX + x] = jnp.concatenate([power, jnp.zeros_like(power)], 0)
    next_y = lax.rem(y + 1, n_y)
    for k in (2, 1, 3, 0):
        px = lax.rem(x + k, NX)

        @pl.when(y < n_y - 1)
        def _():
            send(power_x.at[NX + x], power_x.at[x], 7, {"ctx": next_y * NX + px})

        if k:
            send(power_x.at[NX + x], power_x.at[NX + x], 6, {"ctx": y * NX + px})

    @pl.when(y < n_y - 1)
    def _():
        send(value_row, value_old, 13, {"ctx": next_row}, 8)

    for px in range(NX):
        src, dst = value_row.at[pl.ds(0, px + 1)], value_all.at[pl.ds(SPAN - px, px + 1), x]

        @pl.when(x != px)
        def _():
            send(src, dst, 8 + x, {"ctx": y * NX + px}, 9 + px)

        @pl.when(x == px)
        def _():
            pltpu.make_async_copy(src, dst, recv_sems.at[8 + x]).start()

    received(power_x.at[pl.ds(0, NX - 1)], 6)

    @pl.when(y > 0)
    def _():
        received(power_x.at[pl.ds(0, NX)], 7)

    totals = []
    for half in range(2):
        total = power_x[half * NX]
        for k in range(1, NX):
            total = total + power_x[half * NX + k]
        totals.append(total[:NX])
    power_mp[mp] = jnp.concatenate(totals, 0)

    def share_power(k, carry):
        send(power_mp.at[mp], power_mp.at[mp], 12, {"mp": mp_peer(k)}, 13)
        return carry

    lax.fori_loop(0, n_mp - 1, share_power, 0)

    @pl.when(y > 0)
    def _():
        received(value_old, 13)

    for px in range(NX):
        src, dst = value_old.at[pl.ds(px, NX - px)], value_all.at[pl.ds(0, NX - px), x]

        @pl.when(x != px)
        def _():
            send(src, dst, 8 + x, {"ctx": y * NX + px}, 14 + px)

        @pl.when(x == px)
        def _():
            pltpu.make_async_copy(src, dst, recv_sems.at[8 + x]).start()

    received(key_all.at[pl.ds(0, (NX - 1) * ROWS)], 4)
    reach = (SPAN + 1) * ROWS
    key_at = lax.broadcasted_iota(jnp.int32, (reach, ROWS), 0)
    query_at = lax.broadcasted_iota(jnp.int32, (reach, ROWS), 1)
    first_key = jnp.maximum(SPAN - me, 0) * ROWS
    allowed = (key_at > query_at) & (key_at <= query_at + SPAN * ROWS) & (key_at >= first_key)
    for h in range(NX):
        lanes = pl.ds(h * HEAD, HEAD)
        scores = lax.dot_general(
            key_all[:, lanes], query_ref[:, lanes], (((1,), (1,)), ((), ())), preferred_element_type=F32
        ) * (1.0 / math.sqrt(HEAD))
        scores = jnp.where(allowed, scores, -1e30)
        weights = jnp.exp(scores - jnp.max(scores, 0, keepdims=True))
        denoms[h] = jnp.broadcast_to(jnp.sum(weights, 0, keepdims=True), (8, ROWS))
        probs[h] = weights.astype(BF16)

    for h in range(NX):
        received(value_all.at[:, h], 8 + h)
        mixer_out[:, pl.ds(h * HEAD, HEAD)] = value_all[SPAN, h].astype(F32).T.astype(BF16)

    sent(recv_taps.at[remote_rows], 0)
    sent(recv_signal.at[remote_rows], 1)
    sent(gate_head.at[pl.ds(0, NX - 1)], 2)
    @pl.when(y < n_y - 1)
    def _():
        sent(oldest_keys, 3)
        sent(power_x.at[pl.ds(0, NX)], 7)
        sent(value_row, 8)

    sent(key_all.at[pl.ds(0, (NX - 1) * ROWS)], 4)
    sent(back_send.at[pl.ds(0, (n_y - 1) * NX)], 5)
    sent(power_x.at[pl.ds(0, NX - 1)], 6)
    for px in range(NX):
        @pl.when(x != px)
        def _():
            sent(value_row.at[pl.ds(0, px + 1)], 9 + px)
            sent(value_row.at[pl.ds(0, NX - px)], 14 + px)
    sent(power_mp.at[pl.ds(0, n_mp - 1)], 13)

    received(power_mp.at[pl.ds(0, n_mp - 1)], 12)
    scales[...] = lax.rsqrt(jnp.sum(power_mp[...], 0) * (1.0 / model) + 1e-06)


def attend(mixer_from, value_all, probs, denoms, scales, mixer_to, attended_to, attended, sems):
    x = lax.rem(lax.axis_index("ctx"), NX)
    copies = [pltpu.make_async_copy(mixer_from, mixer_to, sems.at[NX])]
    copies[0].start()
    for h in range(NX):
        values = [
            (value_all[j, h].astype(F32) * scales[pl.ds(x + j, 1), :]).astype(BF16) for j in range(SPAN + 1)
        ]
        summed = jnp.dot(jnp.concatenate(values, 1), probs[h], preferred_element_type=F32)
        lanes = pl.ds(h * HEAD, HEAD)
        attended[:, lanes] = (summed / denoms[h][0:1]).T.astype(BF16)
        copies.append(pltpu.make_async_copy(attended.at[:, lanes], attended_to.at[:, lanes], sems.at[h]))
        copies[-1].start()
    for copy in copies:
        copy.wait()


def solution(mesh):
    blocks, n_mp = mesh.shape["ctx"], mesh.shape["mp"]
    constants = tables(blocks)

    def local(gate_in, value_in, gate_out, filter_taps, skip_gain, queries, key_rows):
        rows, lanes = gate_in.shape
        width = lanes // blocks
        n_y = blocks // NX
        hbm = pl.BlockSpec(memory_space=pltpu.HBM)
        square = (NX, ROWS, HEAD)
        operands = gate_in, value_in, gate_out, filter_taps, queries, key_rows, skip_gain, *constants
        operands = [pltpu.with_memory_space_constraint(o, pltpu.HBM) for o in operands]
        held = pl.pallas_call(
            functools.partial(kernel, blocks, n_mp, n_mp * lanes),
            out_shape=(
                pltpu.VMEM((rows, lanes), BF16),
                pltpu.VMEM((SPAN + 1, NX, HEAD, ROWS), BF16),
                pltpu.VMEM((NX, (SPAN + 1) * ROWS, ROWS), BF16),
                pltpu.VMEM((NX, 8, ROWS), F32),
                pltpu.VMEM((8, ROWS), F32),
            ),
            in_specs=[hbm] * 12,
            out_specs=(pl.BlockSpec(memory_space=pltpu.VMEM),) * 5,
            scratch_shapes=[
                *(pltpu.VMEM((rows, lanes), BF16),) * 3,
                pltpu.VMEM((rows, lanes), F32),
                pltpu.VMEM((rows, lanes), BF16),
                pltpu.SMEM((lanes,), F32),
                *(pltpu.VMEM(c.shape, c.dtype) for c in constants),
                *(pltpu.VMEM((lanes, ROWS), BF16),) * 5,
                pltpu.VMEM((lanes + width, ROWS), F32),
                pltpu.VMEM((lanes, 2 * ROWS), F32),
                pltpu.VMEM(square, BF16),
                pltpu.VMEM((blocks, width, ROWS), BF16),
                pltpu.VMEM((NX, n_y, width, ROWS), BF16),
                pltpu.VMEM(((SPAN + 1) * ROWS, lanes), BF16),
                pltpu.VMEM(square, BF16),
                pltpu.VMEM(square, BF16),
                pltpu.VMEM((2 * NX, 8, ROWS), F32),
                pltpu.VMEM((n_mp, 8, ROWS), F32),
                pltpu.SemaphoreType.DMA((14,)),
                pltpu.SemaphoreType.DMA((18,)),
                pltpu.SemaphoreType.DMA((14,)),
            ],
            compiler_params=pltpu.CompilerParams(
                collective_id=0, has_side_effects=True, vmem_limit_bytes=32 * 2**20
            ),
            cost_estimate=pl.CostEstimate(flops=2 * 10**9, bytes_accessed=2 * 10**6, transcendentals=4 * 10**5),
        )(*operands)
        return pl.pallas_call(
            attend,
            out_shape=(jax.ShapeDtypeStruct((rows, lanes), BF16),) * 2,
            in_specs=[pl.BlockSpec(memory_space=pltpu.VMEM)] * 5,
            out_specs=(hbm,) * 2,
            scratch_shapes=[pltpu.VMEM((rows, lanes), BF16), pltpu.SemaphoreType.DMA((NX + 1,))],
            compiler_params=pltpu.CompilerParams(vmem_limit_bytes=8 * 2**20),
        )(*held)

    return jax.shard_map(
        local,
        mesh=mesh,
        in_specs=(P("ctx", "mp"),) * 4 + (P("mp"),) + (P("ctx", "mp"),) * 2,
        out_specs=(P("ctx", "mp"), P("ctx", "mp")),
        check_vma=False,
    )
```

```python
import functools
import math

import jax
import jax.numpy as jnp
import ml_dtypes
import numpy as np
from jax import lax
from jax.experimental import pallas as pl
from jax.experimental.pallas import tpu as pltpu
from jax.sharding import PartitionSpec as P

HEAD = 128
ROWS = 128
SPAN = 4
NX = 4
MESH = pl.DeviceIdType.MESH
F32 = jnp.float32
BF16 = jnp.bfloat16


def split(table):
    high = table.astype(np.float32).astype(ml_dtypes.bfloat16)
    low = (table - high.astype(np.float64)).astype(np.float32).astype(ml_dtypes.bfloat16)
    return high, low


def tables(blocks):
    length = blocks * ROWS
    n1 = np.arange(blocks)[None, :]
    k1 = np.arange(blocks)[:, None] + 0.25
    n2 = np.arange(ROWS)[None, :]
    first = np.exp(-2j * np.pi * n1 * k1 / blocks)
    twist = np.exp(-2j * np.pi * n2 * k1 / length)
    second = np.exp(-2j * np.pi * n2 * n2.T / ROWS)
    first_high, first_low = split(np.concatenate([first.real, first.imag], 0))
    first_cat = np.concatenate([first_high, first_low], 1)
    wide = np.block([[second.real, second.imag], [-second.imag, second.real]])
    wide_high, wide_low = split(wide)
    last_high, last_low = split(np.concatenate([first.real, first.imag], 0).T / length)
    last_cat = np.concatenate([last_high, last_low, last_high], 1)
    twists = np.stack([twist.real, twist.imag]).astype(np.float32)
    return first_cat, twists, wide_high, wide_low, last_cat


def halves(value):
    high = value.astype(BF16)
    return high, (value - high.astype(F32)).astype(BF16)


def kernel(
    blocks, n_mp, model,
    gate_hbm, value_hbm, out_gate_hbm, taps_hbm, query_hbm, key_hbm, skip_hbm,
    first_hbm, twist_hbm, wide_high_hbm, wide_low_hbm, last_hbm,
    mixer_out, value_all, probs, denoms, scales,
    gate_ref, value_ref, out_gate_ref, taps_ref, query_ref, skip_ref,
    first_ref, twist_ref, wide_high_ref, wide_low_ref, last_ref,
    send_taps, send_signal, send_gate, recv_taps, recv_signal, work, spectrum,
    gate_head, back_send, back_recv, key_all, value_row, value_old,
    power_x, power_mp,
    local_sems, send_sems, recv_sems,
):
    me = lax.axis_index("ctx")
    mp = lax.axis_index("mp")
    x, y = lax.rem(me, NX), lax.div(me, NX)
    n_y = blocks // NX
    width = NX * HEAD // blocks

    def far_first(k, count):
        half = lax.div(k + 1, 2)
        return lax.rem(count // 2 + jnp.where(lax.rem(k, 2) == 1, half, count - half), count)

    def ctx_peer(k):
        px = lax.rem(x + far_first(lax.rem(k, NX), NX), NX)
        py = lax.rem(y + far_first(lax.div(k, NX), n_y), n_y)
        return py * NX + px

    def mp_peer(k):
        return lax.rem(mp + far_first(k, n_mp), n_mp)

    barrier = pltpu.get_barrier_semaphore()

    def greet_ctx(k, carry):
        pl.semaphore_signal(barrier, inc=1, device_id={"ctx": ctx_peer(k)}, device_id_type=MESH)
        return carry

    def greet_mp(k, carry):
        pl.semaphore_signal(barrier, inc=1, device_id={"mp": mp_peer(k)}, device_id_type=MESH)
        return carry

    def fetch(src, dst, which):
        copy = pltpu.make_async_copy(src, dst, local_sems.at[which])
        copy.start()
        return copy

    first_loads = [
        fetch(src, dst, which)
        for which, (src, dst) in enumerate([(taps_hbm, taps_ref), (gate_hbm, gate_ref), (value_hbm, value_ref)])
    ]
    lax.fori_loop(0, blocks - 1, greet_ctx, 0)
    lax.fori_loop(0, n_mp - 1, greet_mp, 0)
    own_rows = pl.ds(SPAN * ROWS, ROWS)
    loads = [
        fetch(src, dst, 3 + which)
        for which, (src, dst) in enumerate([
            (out_gate_hbm, out_gate_ref), (first_hbm, first_ref), (twist_hbm, twist_ref),
            (wide_high_hbm, wide_high_ref), (wide_low_hbm, wide_low_ref), (last_hbm, last_ref), (skip_hbm, skip_ref),
            (query_hbm, query_ref), (key_hbm, key_all.at[own_rows]),
        ])
    ]

    def send(src, dst, which, target, send_which=None):
        pltpu.make_async_remote_copy(
            src_ref=src, dst_ref=dst, send_sem=send_sems.at[which if send_which is None else send_which],
            recv_sem=recv_sems.at[which], device_id=target, device_id_type=MESH,
        ).start()

    def received(ref, which):
        pltpu.make_async_copy(ref, ref, recv_sems.at[which]).wait()

    def sent(ref, which):
        pltpu.make_async_copy(ref, ref, send_sems.at[which]).wait()

    def group(d):
        return pl.ds(pl.multiple_of(lax.rem(d, NX) * HEAD + lax.div(d, NX) * width, width), width)

    mine = pl.ds(pl.multiple_of(me * width, width), width)
    my_lanes = pl.ds(pl.multiple_of(x * HEAD, HEAD), HEAD)

    first_loads[0].wait()
    send_taps[...] = taps_ref[...].T.astype(BF16)
    first_loads[1].wait()
    first_loads[2].wait()
    send_signal[...] = (gate_ref[...].astype(F32) * value_ref[...].astype(F32)).T.astype(BF16)
    pl.semaphore_wait(barrier, blocks - 1 + n_mp - 1)

    def spread(which, src, dst):
        def step(k, carry):
            d = ctx_peer(k)
            send(src.at[group(d)], dst.at[mine], which, {"ctx": d})
            return carry
        lax.fori_loop(0, blocks - 1, step, 0)
        dst[mine] = src[group(me)]

    spread(0, send_taps, recv_taps)
    spread(1, send_signal, recv_signal)

    loads[-1].wait()
    next_row = lax.rem(me + NX, blocks)
    own_keys, oldest_keys = key_all.at[own_rows], key_all.at[pl.ds(0, ROWS)]
    @pl.when(y < n_y - 1)
    def _():
        send(own_keys, oldest_keys, 3, {"ctx": next_row})

    for px in range(1, NX):
        @pl.when(x < px)
        def _():
            slot = pl.multiple_of((SPAN + x - px) * ROWS, ROWS)
            send(own_keys, key_all.at[pl.ds(slot, ROWS)], 4, {"ctx": y * NX + px})

    @pl.when(y == 0)
    def _():
        value_old[...] = jnp.zeros_like(value_old)
        power_x[pl.ds(0, NX)] = jnp.zeros((NX, 8, ROWS), F32)

    loads[0].wait()
    send_gate[...] = out_gate_ref[...].astype(F32).T.astype(BF16)
    for k in (2, 1, 3):
        px = lax.rem(x + k, NX)
        lanes = pl.ds(pl.multiple_of(px * HEAD, HEAD), HEAD)
        send(send_gate.at[lanes], gate_head.at[x], 2, {"ctx": y * NX + px})
    gate_head[x] = send_gate[my_lanes]

    for load in loads[1:-1]:
        load.wait()
    twist_real, twist_imag = twist_ref[0], twist_ref[1]

    def times_wide(value, contract):
        high, low = halves(value)
        dims = (((1,), (contract,)), ((), ()))

        def dot(a, b):
            return lax.dot_general(a, b, dims, preferred_element_type=F32)

        return dot(high, wide_high_ref[...]) + dot(low, wide_high_ref[...]) + dot(high, wide_low_ref[...])

    def lane_tile(value, c):
        return value[:, c * ROWS:(c + 1) * ROWS]

    def forward(recv):
        work[all_rows] = recv[...].astype(F32)
        panel = jnp.concatenate([work[pl.ds(c, blocks, stride=width), :] for c in range(width)], 1).astype(BF16)
        panel = jnp.concatenate([panel, panel], 0)
        bins = jnp.dot(first_ref[...], panel, preferred_element_type=F32)
        real, imag = bins[:blocks], bins[blocks:]
        rows = []
        for c in range(width):
            a, b = lane_tile(real, c), lane_tile(imag, c)
            rows.append(jnp.concatenate([a * twist_real - b * twist_imag, a * twist_imag + b * twist_real], 1))
        return times_wide(jnp.concatenate(rows, 0), 0)

    remote_rows, all_rows = pl.ds(0, (blocks - 1) * width), pl.ds(0, blocks * width)
    received(recv_taps.at[remote_rows], 0)
    spectrum[...] = forward(recv_taps)
    skip_at = x * HEAD + y * width
    for c in range(width):
        rows = pl.ds(c * blocks, blocks)
        spectrum[rows, pl.ds(0, ROWS)] = spectrum[rows, pl.ds(0, ROWS)] + skip_ref[skip_at + c]
    received(recv_signal.at[remote_rows], 1)

    bins = forward(recv_signal)
    a, b = bins[:, :ROWS], bins[:, ROWS:]
    c, d = spectrum[:, pl.ds(0, ROWS)], spectrum[:, pl.ds(ROWS, ROWS)]
    back = times_wide(jnp.concatenate([a * c - b * d, a * d + b * c], 1), 1)
    columns = []
    for c in range(width):
        part = back[c * blocks:(c + 1) * blocks]
        a, b = part[:, :ROWS], part[:, ROWS:]
        columns.append(jnp.concatenate([a * twist_real + b * twist_imag, b * twist_real - a * twist_imag], 0))
    high, low = halves(jnp.concatenate(columns, 1))
    convolved = jnp.dot(last_ref[...], jnp.concatenate([high, high, low], 0), preferred_element_type=F32)
    for c in range(width):
        work[pl.ds(c, blocks, stride=width), :] = lane_tile(convolved, c)
    back_send[...] = work[all_rows].astype(BF16).reshape(blocks, width, ROWS)

    def send_back(k, carry):
        py = lax.rem(y + far_first(k, n_y), n_y)
        send(back_send.at[pl.ds(py * NX, NX)], back_recv.at[:, y], 5, {"ctx": py * NX + x})
        return carry

    lax.fori_loop(0, n_y - 1, send_back, 0)
    back_recv[:, y] = back_send[pl.ds(y * NX, NX)]

    @pl.when(y > 0)
    def _():
        received(oldest_keys, 3)

    for px in range(NX - 1):
        @pl.when(x > px)
        def _():
            slot = pl.multiple_of((x - px) * ROWS, ROWS)
            send(oldest_keys, key_all.at[pl.ds(slot, ROWS)], 4, {"ctx": y * NX + px})

    received(gate_head.at[pl.ds(0, NX - 1)], 2)
    received(back_send.at[pl.ds(0, (n_y - 1) * NX)], 5)
    gated = gate_head[...].astype(F32) * back_recv[...].reshape(NX, HEAD, ROWS).astype(F32)
    mixed = gated.astype(BF16)
    value_row[...] = mixed
    widened = mixed.astype(F32)
    power = jnp.sum(widened * widened, 1)
    power_x[NX + x] = jnp.concatenate([power, jnp.zeros_like(power)], 0)
    next_y = lax.rem(y + 1, n_y)
    for k in (2, 1, 3, 0):
        px = lax.rem(x + k, NX)

        @pl.when(y < n_y - 1)
        def _():
            send(power_x.at[NX + x], power_x.at[x], 7, {"ctx": next_y * NX + px})

        if k:
            send(power_x.at[NX + x], power_x.at[NX + x], 6, {"ctx": y * NX + px})

    @pl.when(y < n_y - 1)
    def _():
        for half in (1, 0):
            part = pl.ds(2 * half, 2)
            send(value_row.at[part], value_old.at[part], 13 + half, {"ctx": next_row}, 8 + 10 * half)

    for px in range(NX):
        src, dst = value_row.at[pl.ds(0, px + 1)], value_all.at[pl.ds(SPAN - px, px + 1), x]

        @pl.when(x != px)
        def _():
            send(src, dst, 8 + x, {"ctx": y * NX + px}, 9 + px)

        @pl.when(x == px)
        def _():
            pltpu.make_async_copy(src, dst, recv_sems.at[8 + x]).start()

    received(power_x.at[pl.ds(0, NX - 1)], 6)

    @pl.when(y > 0)
    def _():
        received(power_x.at[pl.ds(0, NX)], 7)

    totals = []
    for half in range(2):
        total = power_x[half * NX]
        for k in range(1, NX):
            total = total + power_x[half * NX + k]
        totals.append(total[:NX])
    power_mp[mp] = jnp.concatenate(totals, 0)

    def share_power(k, carry):
        send(power_mp.at[mp], power_mp.at[mp], 12, {"mp": mp_peer(k)}, 13)
        return carry

    lax.fori_loop(0, n_mp - 1, share_power, 0)

    for half in (1, 0):
        @pl.when(y > 0)
        def _():
            received(value_old.at[pl.ds(2 * half, 2)], 13 + half)

        for px in range(2 * half + 2):
            first = max(px, 2 * half)
            count = 2 * half + 2 - first
            src, dst = value_old.at[pl.ds(first, count)], value_all.at[pl.ds(first - px, count), x]

            @pl.when(x != px)
            def _():
                send(src, dst, 8 + x, {"ctx": y * NX + px}, 14 + px)

            @pl.when(x == px)
            def _():
                pltpu.make_async_copy(src, dst, recv_sems.at[8 + x]).start()

    received(key_all.at[pl.ds(0, (NX - 1) * ROWS)], 4)
    reach = (SPAN + 1) * ROWS
    key_at = lax.broadcasted_iota(jnp.int32, (reach, ROWS), 0)
    query_at = lax.broadcasted_iota(jnp.int32, (reach, ROWS), 1)
    first_key = jnp.maximum(SPAN - me, 0) * ROWS
    allowed = (key_at > query_at) & (key_at <= query_at + SPAN * ROWS) & (key_at >= first_key)
    for h in range(NX):
        lanes = pl.ds(h * HEAD, HEAD)
        scores = lax.dot_general(
            key_all[:, lanes], query_ref[:, lanes], (((1,), (1,)), ((), ())), preferred_element_type=F32
        ) * (1.0 / math.sqrt(HEAD))
        scores = jnp.where(allowed, scores, -1e30)
        weights = jnp.exp(scores - jnp.max(scores, 0, keepdims=True))
        denoms[h] = jnp.broadcast_to(jnp.sum(weights, 0, keepdims=True), (8, ROWS))
        probs[h] = weights.astype(BF16)

    for h in range(NX):
        received(value_all.at[:, h], 8 + h)
        mixer_out[:, pl.ds(h * HEAD, HEAD)] = value_all[SPAN, h].astype(F32).T.astype(BF16)

    sent(recv_taps.at[remote_rows], 0)
    sent(recv_signal.at[remote_rows], 1)
    sent(gate_head.at[pl.ds(0, NX - 1)], 2)
    @pl.when(y < n_y - 1)
    def _():
        sent(oldest_keys, 3)
        sent(power_x.at[pl.ds(0, NX)], 7)
        sent(value_row.at[pl.ds(0, 2)], 8)
        sent(value_row.at[pl.ds(2, 2)], 18)

    sent(key_all.at[pl.ds(0, (NX - 1) * ROWS)], 4)
    sent(back_send.at[pl.ds(0, (n_y - 1) * NX)], 5)
    sent(power_x.at[pl.ds(0, NX - 1)], 6)
    for px in range(NX):
        @pl.when(x != px)
        def _():
            sent(value_row.at[pl.ds(0, px + 1)], 9 + px)
            sent(value_row.at[pl.ds(0, NX - px)], 14 + px)
    sent(power_mp.at[pl.ds(0, n_mp - 1)], 13)

    received(power_mp.at[pl.ds(0, n_mp - 1)], 12)
    scales[...] = lax.rsqrt(jnp.sum(power_mp[...], 0) * (1.0 / model) + 1e-06)


def attend(mixer_from, value_all, probs, denoms, scales, mixer_to, attended_to, attended, sems):
    x = lax.rem(lax.axis_index("ctx"), NX)
    copies = []
    for h in range(NX):
        values = [
            (value_all[j, h].astype(F32) * scales[pl.ds(x + j, 1), :]).astype(BF16) for j in range(SPAN + 1)
        ]
        summed = jnp.dot(jnp.concatenate(values, 1), probs[h], preferred_element_type=F32)
        lanes = pl.ds(h * HEAD, HEAD)
        attended[:, lanes] = (summed / denoms[h][0:1]).T.astype(BF16)
        copies.append(pltpu.make_async_copy(attended.at[:, lanes], attended_to.at[:, lanes], sems.at[h]))
        copies[-1].start()
        if h == 0:
            copies.append(pltpu.make_async_copy(mixer_from, mixer_to, sems.at[NX]))
            copies[-1].start()
    for copy in copies:
        copy.wait()


def solution(mesh):
    blocks, n_mp = mesh.shape["ctx"], mesh.shape["mp"]
    constants = tables(blocks)

    def local(gate_in, value_in, gate_out, filter_taps, skip_gain, queries, key_rows):
        rows, lanes = gate_in.shape
        width = lanes // blocks
        n_y = blocks // NX
        hbm = pl.BlockSpec(memory_space=pltpu.HBM)
        square = (NX, ROWS, HEAD)
        operands = gate_in, value_in, gate_out, filter_taps, queries, key_rows, skip_gain, *constants
        operands = [pltpu.with_memory_space_constraint(o, pltpu.HBM) for o in operands]
        held = pl.pallas_call(
            functools.partial(kernel, blocks, n_mp, n_mp * lanes),
            out_shape=(
                pltpu.VMEM((rows, lanes), BF16),
                pltpu.VMEM((SPAN + 1, NX, HEAD, ROWS), BF16),
                pltpu.VMEM((NX, (SPAN + 1) * ROWS, ROWS), BF16),
                pltpu.VMEM((NX, 8, ROWS), F32),
                pltpu.VMEM((8, ROWS), F32),
            ),
            in_specs=[hbm] * 12,
            out_specs=(pl.BlockSpec(memory_space=pltpu.VMEM),) * 5,
            scratch_shapes=[
                *(pltpu.VMEM((rows, lanes), BF16),) * 3,
                pltpu.VMEM((rows, lanes), F32),
                pltpu.VMEM((rows, lanes), BF16),
                pltpu.SMEM((lanes,), F32),
                *(pltpu.VMEM(c.shape, c.dtype) for c in constants),
                *(pltpu.VMEM((lanes, ROWS), BF16),) * 5,
                pltpu.VMEM((lanes + width, ROWS), F32),
                pltpu.VMEM((lanes, 2 * ROWS), F32),
                pltpu.VMEM(square, BF16),
                pltpu.VMEM((blocks, width, ROWS), BF16),
                pltpu.VMEM((NX, n_y, width, ROWS), BF16),
                pltpu.VMEM(((SPAN + 1) * ROWS, lanes), BF16),
                pltpu.VMEM(square, BF16),
                pltpu.VMEM(square, BF16),
                pltpu.VMEM((2 * NX, 8, ROWS), F32),
                pltpu.VMEM((n_mp, 8, ROWS), F32),
                pltpu.SemaphoreType.DMA((14,)),
                pltpu.SemaphoreType.DMA((19,)),
                pltpu.SemaphoreType.DMA((15,)),
            ],
            compiler_params=pltpu.CompilerParams(
                collective_id=0, has_side_effects=True, vmem_limit_bytes=32 * 2**20
            ),
            cost_estimate=pl.CostEstimate(flops=2 * 10**9, bytes_accessed=2 * 10**6, transcendentals=4 * 10**5),
        )(*operands)
        return pl.pallas_call(
            attend,
            out_shape=(jax.ShapeDtypeStruct((rows, lanes), BF16),) * 2,
            in_specs=[pl.BlockSpec(memory_space=pltpu.VMEM)] * 5,
            out_specs=(hbm,) * 2,
            scratch_shapes=[pltpu.VMEM((rows, lanes), BF16), pltpu.SemaphoreType.DMA((NX + 1,))],
            compiler_params=pltpu.CompilerParams(vmem_limit_bytes=8 * 2**20),
        )(*held)

    return jax.shard_map(
        local,
        mesh=mesh,
        in_specs=(P("ctx", "mp"),) * 4 + (P("mp"),) + (P("ctx", "mp"),) * 2,
        out_specs=(P("ctx", "mp"), P("ctx", "mp")),
        check_vma=False,
    )
```

```python
import functools
import math

import jax
import jax.numpy as jnp
import ml_dtypes
import numpy as np
from jax import lax
from jax.experimental import pallas as pl
from jax.experimental.pallas import tpu as pltpu
from jax.sharding import PartitionSpec as P

HEAD = 128
ROWS = 128
SPAN = 4
NX = 4
MESH = pl.DeviceIdType.MESH
F32 = jnp.float32
BF16 = jnp.bfloat16


def split(table):
    high = table.astype(np.float32).astype(ml_dtypes.bfloat16)
    low = (table - high.astype(np.float64)).astype(np.float32).astype(ml_dtypes.bfloat16)
    return high, low


def tables(blocks):
    length = blocks * ROWS
    n1 = np.arange(blocks)[None, :]
    k1 = np.arange(blocks)[:, None] + 0.25
    n2 = np.arange(ROWS)[None, :]
    first = np.exp(-2j * np.pi * n1 * k1 / blocks)
    twist = np.exp(-2j * np.pi * n2 * k1 / length)
    second = np.exp(-2j * np.pi * n2 * n2.T / ROWS)
    first_high, first_low = split(np.concatenate([first.real, first.imag], 0))
    first_cat = np.concatenate([first_high, first_low], 1)
    wide = np.block([[second.real, second.imag], [-second.imag, second.real]])
    wide_high, wide_low = split(wide)
    last_high, last_low = split(np.concatenate([first.real, first.imag], 0).T / length)
    last_cat = np.concatenate([last_high, last_low, last_high], 1)
    twists = np.stack([twist.real, twist.imag]).astype(np.float32)
    return first_cat, twists, wide_high, wide_low, last_cat


def halves(value):
    high = value.astype(BF16)
    return high, (value - high.astype(F32)).astype(BF16)


def kernel(
    blocks, n_mp, model,
    gate_hbm, value_hbm, out_gate_hbm, taps_hbm, query_hbm, key_hbm, skip_hbm,
    first_hbm, twist_hbm, wide_high_hbm, wide_low_hbm, last_hbm,
    mixer_out, value_all, probs, denoms, scales,
    gate_ref, value_ref, out_gate_ref, taps_ref, query_ref, skip_ref,
    first_ref, twist_ref, wide_high_ref, wide_low_ref, last_ref,
    send_taps, send_signal, send_gate, recv_taps, recv_signal, work, spectrum,
    gate_head, back_send, back_recv, key_all, value_row, value_old,
    power_x, power_mp,
    local_sems, send_sems, recv_sems,
):
    me = lax.axis_index("ctx")
    mp = lax.axis_index("mp")
    x, y = lax.rem(me, NX), lax.div(me, NX)
    n_y = blocks // NX
    width = NX * HEAD // blocks

    def far_first(k, count):
        half = lax.div(k + 1, 2)
        return lax.rem(count // 2 + jnp.where(lax.rem(k, 2) == 1, half, count - half), count)

    def ctx_peer(k):
        px = lax.rem(x + far_first(lax.rem(k, NX), NX), NX)
        py = lax.rem(y + far_first(lax.div(k, NX), n_y), n_y)
        return py * NX + px

    def mp_peer(k):
        return lax.rem(mp + far_first(k, n_mp), n_mp)

    barrier = pltpu.get_barrier_semaphore()

    def greet_ctx(k, carry):
        pl.semaphore_signal(barrier, inc=1, device_id={"ctx": ctx_peer(k)}, device_id_type=MESH)
        return carry

    def greet_mp(k, carry):
        pl.semaphore_signal(barrier, inc=1, device_id={"mp": mp_peer(k)}, device_id_type=MESH)
        return carry

    def fetch(src, dst, which):
        copy = pltpu.make_async_copy(src, dst, local_sems.at[which])
        copy.start()
        return copy

    first_loads = [
        fetch(src, dst, which)
        for which, (src, dst) in enumerate([(taps_hbm, taps_ref), (gate_hbm, gate_ref), (value_hbm, value_ref)])
    ]
    lax.fori_loop(0, blocks - 1, greet_ctx, 0)
    lax.fori_loop(0, n_mp - 1, greet_mp, 0)
    own_rows = pl.ds(SPAN * ROWS, ROWS)
    loads = [
        fetch(src, dst, 3 + which)
        for which, (src, dst) in enumerate([
            (out_gate_hbm, out_gate_ref), (first_hbm, first_ref), (twist_hbm, twist_ref),
            (wide_high_hbm, wide_high_ref), (wide_low_hbm, wide_low_ref), (last_hbm, last_ref), (skip_hbm, skip_ref),
            (query_hbm, query_ref), (key_hbm, key_all.at[own_rows]),
        ])
    ]

    def send(src, dst, which, target, send_which=None):
        pltpu.make_async_remote_copy(
            src_ref=src, dst_ref=dst, send_sem=send_sems.at[which if send_which is None else send_which],
            recv_sem=recv_sems.at[which], device_id=target, device_id_type=MESH,
        ).start()

    def received(ref, which):
        pltpu.make_async_copy(ref, ref, recv_sems.at[which]).wait()

    def sent(ref, which):
        pltpu.make_async_copy(ref, ref, send_sems.at[which]).wait()

    def group(d):
        return pl.ds(pl.multiple_of(lax.rem(d, NX) * HEAD + lax.div(d, NX) * width, width), width)

    mine = pl.ds(pl.multiple_of(me * width, width), width)
    my_lanes = pl.ds(pl.multiple_of(x * HEAD, HEAD), HEAD)

    first_loads[0].wait()
    send_taps[...] = taps_ref[...].T.astype(BF16)
    first_loads[1].wait()
    first_loads[2].wait()
    send_signal[...] = (gate_ref[...].astype(F32) * value_ref[...].astype(F32)).T.astype(BF16)
    pl.semaphore_wait(barrier, blocks - 1 + n_mp - 1)

    def spread(which, src, dst):
        def step(k, carry):
            d = ctx_peer(k)
            send(src.at[group(d)], dst.at[mine], which, {"ctx": d})
            return carry
        lax.fori_loop(0, blocks - 1, step, 0)
        dst[mine] = src[group(me)]

    spread(0, send_taps, recv_taps)
    spread(1, send_signal, recv_signal)

    loads[-1].wait()
    next_row = lax.rem(me + NX, blocks)
    own_keys, oldest_keys = key_all.at[own_rows], key_all.at[pl.ds(0, ROWS)]
    @pl.when(y < n_y - 1)
    def _():
        send(own_keys, oldest_keys, 3, {"ctx": next_row})

    for px in range(1, NX):
        @pl.when(x < px)
        def _():
            slot = pl.multiple_of((SPAN + x - px) * ROWS, ROWS)
            send(own_keys, key_all.at[pl.ds(slot, ROWS)], 4, {"ctx": y * NX + px})

    @pl.when(y == 0)
    def _():
        value_old[...] = jnp.zeros_like(value_old)
        power_x[pl.ds(0, NX)] = jnp.zeros((NX, 8, ROWS), F32)

    loads[0].wait()
    send_gate[...] = out_gate_ref[...].astype(F32).T.astype(BF16)
    for k in (2, 1, 3):
        px = lax.rem(x + k, NX)
        lanes = pl.ds(pl.multiple_of(px * HEAD, HEAD), HEAD)
        send(send_gate.at[lanes], gate_head.at[x], 2, {"ctx": y * NX + px})
    gate_head[x] = send_gate[my_lanes]

    for load in loads[1:-1]:
        load.wait()
    twist_real, twist_imag = twist_ref[0], twist_ref[1]

    def times_wide(value, contract):
        high, low = halves(value)
        dims = (((1,), (contract,)), ((), ()))

        def dot(a, b):
            return lax.dot_general(a, b, dims, preferred_element_type=F32)

        return dot(high, wide_high_ref[...]) + dot(low, wide_high_ref[...]) + dot(high, wide_low_ref[...])

    def lane_tile(value, c):
        return value[:, c * ROWS:(c + 1) * ROWS]

    def forward(recv):
        work[all_rows] = recv[...].astype(F32)
        panel = jnp.concatenate([work[pl.ds(c, blocks, stride=width), :] for c in range(width)], 1).astype(BF16)
        panel = jnp.concatenate([panel, panel], 0)
        bins = jnp.dot(first_ref[...], panel, preferred_element_type=F32)
        real, imag = bins[:blocks], bins[blocks:]
        rows = []
        for c in range(width):
            a, b = lane_tile(real, c), lane_tile(imag, c)
            rows.append(jnp.concatenate([a * twist_real - b * twist_imag, a * twist_imag + b * twist_real], 1))
        return times_wide(jnp.concatenate(rows, 0), 0)

    remote_rows, all_rows = pl.ds(0, (blocks - 1) * width), pl.ds(0, blocks * width)
    received(recv_taps.at[remote_rows], 0)
    spectrum[...] = forward(recv_taps)
    skip_at = x * HEAD + y * width
    for c in range(width):
        rows = pl.ds(c * blocks, blocks)
        spectrum[rows, pl.ds(0, ROWS)] = spectrum[rows, pl.ds(0, ROWS)] + skip_ref[skip_at + c]
    received(recv_signal.at[remote_rows], 1)

    bins = forward(recv_signal)
    a, b = bins[:, :ROWS], bins[:, ROWS:]
    c, d = spectrum[:, pl.ds(0, ROWS)], spectrum[:, pl.ds(ROWS, ROWS)]
    back = times_wide(jnp.concatenate([a * c - b * d, a * d + b * c], 1), 1)
    columns = []
    for c in range(width):
        part = back[c * blocks:(c + 1) * blocks]
        a, b = part[:, :ROWS], part[:, ROWS:]
        columns.append(jnp.concatenate([a * twist_real + b * twist_imag, b * twist_real - a * twist_imag], 0))
    high, low = halves(jnp.concatenate(columns, 1))
    convolved = jnp.dot(last_ref[...], jnp.concatenate([high, high, low], 0), preferred_element_type=F32)
    for c in range(width):
        work[pl.ds(c, blocks, stride=width), :] = lane_tile(convolved, c)
    back_send[...] = work[all_rows].astype(BF16).reshape(blocks, width, ROWS)

    def send_back(k, carry):
        py = lax.rem(y + far_first(k, n_y), n_y)
        send(back_send.at[pl.ds(py * NX, NX)], back_recv.at[:, y], 5, {"ctx": py * NX + x})
        return carry

    lax.fori_loop(0, n_y - 1, send_back, 0)
    back_recv[:, y] = back_send[pl.ds(y * NX, NX)]

    @pl.when(y > 0)
    def _():
        received(oldest_keys, 3)

    for px in range(NX - 1):
        @pl.when(x > px)
        def _():
            slot = pl.multiple_of((x - px) * ROWS, ROWS)
            send(oldest_keys, key_all.at[pl.ds(slot, ROWS)], 4, {"ctx": y * NX + px})

    received(gate_head.at[pl.ds(0, NX - 1)], 2)
    received(back_send.at[pl.ds(0, (n_y - 1) * NX)], 5)
    gated = gate_head[...].astype(F32) * back_recv[...].reshape(NX, HEAD, ROWS).astype(F32)
    mixed = gated.astype(BF16)
    value_row[...] = mixed
    widened = mixed.astype(F32)
    power = jnp.sum(widened * widened, 1)
    power_x[NX + x] = jnp.concatenate([power, jnp.zeros_like(power)], 0)
    next_y = lax.rem(y + 1, n_y)
    for k in (2, 1, 3, 0):
        px = lax.rem(x + k, NX)

        @pl.when(y < n_y - 1)
        def _():
            send(power_x.at[NX + x], power_x.at[x], 7, {"ctx": next_y * NX + px})

        if k:
            send(power_x.at[NX + x], power_x.at[NX + x], 6, {"ctx": y * NX + px})

    @pl.when(y < n_y - 1)
    def _():
        send(value_row, value_old, 13, {"ctx": next_row}, 8)

    for px in range(NX):
        src, dst = value_row.at[pl.ds(0, px + 1)], value_all.at[pl.ds(SPAN - px, px + 1), x]

        @pl.when(x != px)
        def _():
            send(src, dst, 8 + x, {"ctx": y * NX + px}, 9 + px)

        @pl.when(x == px)
        def _():
            pltpu.make_async_copy(src, dst, recv_sems.at[8 + x]).start()

    received(power_x.at[pl.ds(0, NX - 1)], 6)

    @pl.when(y > 0)
    def _():
        received(power_x.at[pl.ds(0, NX)], 7)

    totals = []
    for half in range(2):
        total = power_x[half * NX]
        for k in range(1, NX):
            total = total + power_x[half * NX + k]
        totals.append(total[:NX])
    power_mp[mp] = jnp.concatenate(totals, 0)

    def share_power(k, carry):
        send(power_mp.at[mp], power_mp.at[mp], 12, {"mp": mp_peer(k)}, 13)
        return carry

    lax.fori_loop(0, n_mp - 1, share_power, 0)

    @pl.when(y > 0)
    def _():
        received(value_old, 13)

    for px in range(NX):
        src, dst = value_old.at[pl.ds(px, NX - px)], value_all.at[pl.ds(0, NX - px), x]

        @pl.when(x != px)
        def _():
            send(src, dst, 8 + x, {"ctx": y * NX + px}, 14 + px)

        @pl.when(x == px)
        def _():
            pltpu.make_async_copy(src, dst, recv_sems.at[8 + x]).start()

    received(key_all.at[pl.ds(0, (NX - 1) * ROWS)], 4)
    reach = (SPAN + 1) * ROWS
    key_at = lax.broadcasted_iota(jnp.int32, (reach, ROWS), 0)
    query_at = lax.broadcasted_iota(jnp.int32, (reach, ROWS), 1)
    first_key = jnp.maximum(SPAN - me, 0) * ROWS
    allowed = (key_at > query_at) & (key_at <= query_at + SPAN * ROWS) & (key_at >= first_key)
    for h in range(NX):
        lanes = pl.ds(h * HEAD, HEAD)
        scores = lax.dot_general(
            key_all[:, lanes], query_ref[:, lanes], (((1,), (1,)), ((), ())), preferred_element_type=F32
        ) * (1.0 / math.sqrt(HEAD))
        scores = jnp.where(allowed, scores, -1e30)
        weights = jnp.exp(scores - jnp.max(scores, 0, keepdims=True))
        denoms[h] = jnp.broadcast_to(1.0 / jnp.sum(weights, 0, keepdims=True), (8, ROWS))
        probs[h] = weights.astype(BF16)

    for h in range(NX):
        received(value_all.at[:, h], 8 + h)
        mixer_out[:, pl.ds(h * HEAD, HEAD)] = value_all[SPAN, h].astype(F32).T.astype(BF16)

    sent(recv_taps.at[remote_rows], 0)
    sent(recv_signal.at[remote_rows], 1)
    sent(gate_head.at[pl.ds(0, NX - 1)], 2)
    @pl.when(y < n_y - 1)
    def _():
        sent(oldest_keys, 3)
        sent(power_x.at[pl.ds(0, NX)], 7)
        sent(value_row, 8)

    sent(key_all.at[pl.ds(0, (NX - 1) * ROWS)], 4)
    sent(back_send.at[pl.ds(0, (n_y - 1) * NX)], 5)
    sent(power_x.at[pl.ds(0, NX - 1)], 6)
    for px in range(NX):
        @pl.when(x != px)
        def _():
            sent(value_row.at[pl.ds(0, px + 1)], 9 + px)
            sent(value_row.at[pl.ds(0, NX - px)], 14 + px)
    sent(power_mp.at[pl.ds(0, n_mp - 1)], 13)

    received(power_mp.at[pl.ds(0, n_mp - 1)], 12)
    scales[...] = lax.rsqrt(jnp.sum(power_mp[...], 0) * (1.0 / model) + 1e-06)


def attend(mixer_from, value_all, probs, denoms, scales, mixer_to, attended_to, attended, sems):
    x = lax.rem(lax.axis_index("ctx"), NX)
    copies = [pltpu.make_async_copy(mixer_from, mixer_to, sems.at[NX])]
    copies[0].start()
    for h in range(NX):
        values = [
            (value_all[j, h].astype(F32) * scales[pl.ds(x + j, 1), :]).astype(BF16) for j in range(SPAN + 1)
        ]
        summed = jnp.dot(jnp.concatenate(values, 1), probs[h], preferred_element_type=F32)
        lanes = pl.ds(h * HEAD, HEAD)
        attended[:, lanes] = (summed * denoms[h][0:1]).T.astype(BF16)
        copies.append(pltpu.make_async_copy(attended.at[:, lanes], attended_to.at[:, lanes], sems.at[h]))
        copies[-1].start()
    for copy in copies:
        copy.wait()


def solution(mesh):
    blocks, n_mp = mesh.shape["ctx"], mesh.shape["mp"]
    constants = tables(blocks)

    def local(gate_in, value_in, gate_out, filter_taps, skip_gain, queries, key_rows):
        rows, lanes = gate_in.shape
        width = lanes // blocks
        n_y = blocks // NX
        hbm = pl.BlockSpec(memory_space=pltpu.HBM)
        square = (NX, ROWS, HEAD)
        operands = gate_in, value_in, gate_out, filter_taps, queries, key_rows, skip_gain, *constants
        operands = [pltpu.with_memory_space_constraint(o, pltpu.HBM) for o in operands]
        held = pl.pallas_call(
            functools.partial(kernel, blocks, n_mp, n_mp * lanes),
            out_shape=(
                pltpu.VMEM((rows, lanes), BF16),
                pltpu.VMEM((SPAN + 1, NX, HEAD, ROWS), BF16),
                pltpu.VMEM((NX, (SPAN + 1) * ROWS, ROWS), BF16),
                pltpu.VMEM((NX, 8, ROWS), F32),
                pltpu.VMEM((8, ROWS), F32),
            ),
            in_specs=[hbm] * 12,
            out_specs=(pl.BlockSpec(memory_space=pltpu.VMEM),) * 5,
            scratch_shapes=[
                *(pltpu.VMEM((rows, lanes), BF16),) * 3,
                pltpu.VMEM((rows, lanes), F32),
                pltpu.VMEM((rows, lanes), BF16),
                pltpu.SMEM((lanes,), F32),
                *(pltpu.VMEM(c.shape, c.dtype) for c in constants),
                *(pltpu.VMEM((lanes, ROWS), BF16),) * 5,
                pltpu.VMEM((lanes + width, ROWS), F32),
                pltpu.VMEM((lanes, 2 * ROWS), F32),
                pltpu.VMEM(square, BF16),
                pltpu.VMEM((blocks, width, ROWS), BF16),
                pltpu.VMEM((NX, n_y, width, ROWS), BF16),
                pltpu.VMEM(((SPAN + 1) * ROWS, lanes), BF16),
                pltpu.VMEM(square, BF16),
                pltpu.VMEM(square, BF16),
                pltpu.VMEM((2 * NX, 8, ROWS), F32),
                pltpu.VMEM((n_mp, 8, ROWS), F32),
                pltpu.SemaphoreType.DMA((14,)),
                pltpu.SemaphoreType.DMA((18,)),
                pltpu.SemaphoreType.DMA((14,)),
            ],
            compiler_params=pltpu.CompilerParams(
                collective_id=0, has_side_effects=True, vmem_limit_bytes=32 * 2**20
            ),
            cost_estimate=pl.CostEstimate(flops=2 * 10**9, bytes_accessed=2 * 10**6, transcendentals=4 * 10**5),
        )(*operands)
        return pl.pallas_call(
            attend,
            out_shape=(jax.ShapeDtypeStruct((rows, lanes), BF16),) * 2,
            in_specs=[pl.BlockSpec(memory_space=pltpu.VMEM)] * 5,
            out_specs=(hbm,) * 2,
            scratch_shapes=[pltpu.VMEM((rows, lanes), BF16), pltpu.SemaphoreType.DMA((NX + 1,))],
            compiler_params=pltpu.CompilerParams(vmem_limit_bytes=8 * 2**20),
        )(*held)

    return jax.shard_map(
        local,
        mesh=mesh,
        in_specs=(P("ctx", "mp"),) * 4 + (P("mp"),) + (P("ctx", "mp"),) * 2,
        out_specs=(P("ctx", "mp"), P("ctx", "mp")),
        check_vma=False,
    )
```
